256 devices in a mesh: seq: 64 (over y, x, z_hi), head: 4 (over z_lo, core).
Axes of the slice: x: 4, y: 4, z: 8 (z_hi: 4, z_lo: 2; z = z_hi * 2 + z_lo), core: 2. Of those that a mesh axis runs over, the one named last changes fastest.
Arguments:
- tokens: bfloat16 [12288, 3072], P('seq', 'head'), may hold values from -6 to 6
- prompt: bfloat16 [256, 3072], replicated, may hold values from -6 to 6
- prompt_mask: int32 [256], replicated, may hold values from 0 to 1, as said below
- shift_vec: float32 [3072], replicated, may hold values from -3 to 3
- scale_vec: float32 [3072], replicated, may hold values from -2.5 to 2.5
- gate_vec: float32 [3072], P('head'), may hold values from -4 to 4
- qkv_weight: bfloat16 [3072, 4608], P('seq', 'head'), may hold values from -0.109375 to 0.109375
- query_gain: float32 [128], replicated, may hold values from 1.5 to 3
- key_gain: float32 [128], replicated, may hold values from 1.5 to 3
- out_weight: bfloat16 [1536, 3072], P('head', 'seq'), may hold values from -0.15625 to 0.15625
Outputs:
- block_out: bfloat16 [12288, 3072], P('seq', 'head')
The draws below stay inside these ranges and needn't reach their ends.
Inputs may be any that keep to these rules, and one draw needn't show every extreme that they name: `prompt_mask`: 1 on a leading run of at least 64 positions and 0 after it, with at least one 0.
All inputs are finite; a program needn't handle non-finite values.
Results may differ from the reference program's by a relative error of at most 0.012.
The reference program's roundings to bfloat16 on the way (of `inputs`, `probs` and `attended`) count: a program that leaves them out, or rounds other values in their place, can miss the bound.
Values may be sent and summed in bfloat16 or wider, within the bound.
No kernel may reach another device: no remote copies, remote signals or barrier semaphores. Data moves between devices by JAX's collectives and lax.ppermute only.
A program may use at most 128 MiB of HBM per device.

```python
import math
import jax
import jax.numpy as jnp
from jax import lax

D = 3072
HEADS = 12
HD = 128
TEXT = 256
TOKENS = 12288


def draw_prompt_mask(key, part):
    key = jax.random.fold_in(key, 7)
    length = jax.random.randint(key, (), TEXT // 4, TEXT)
    return (jnp.arange(TEXT, dtype=jnp.int32) < length).astype(jnp.int32)


def block_levels(own_key, dims, split, smallest, high):
    loudness = 1.0
    for dim, parts in split:
        heights = jax.random.uniform(jax.random.fold_in(jax.random.fold_in(own_key, 6), dim), (parts,), jnp.float32, smallest / len(split), high / len(split))
        loudness = loudness * jnp.repeat(jnp.exp(heights), dims[dim] // parts).reshape((-1,) + (1,) * (len(dims) - 1 - dim))
    return loudness


def scatter_about(own_key, extent, scale, limit, cuts=(), kind=jnp.bfloat16):
    result = scale * jax.random.normal(own_key, extent, jnp.float32)
    if cuts:
        result = result * block_levels(own_key, extent, cuts, -0.22, 0.18)
    return jnp.clip(result, -limit, limit).astype(kind)


def setup_inputs(seed: int = 0) -> dict:
    seeds = jax.random.split(jax.random.key(seed), 11)
    return {
        "tokens": scatter_about(seeds[0], (TOKENS, D), 1.0, 6.0, ((0, 64), (1, 4))),
        "prompt": scatter_about(seeds[1], (TEXT, D), 1.0, 6.0),
        "prompt_mask": draw_prompt_mask(jax.random.fold_in(seeds[10], 71), 0),
        "shift_vec": scatter_about(seeds[3], (D,), 0.5, 3.0, (), jnp.float32),
        "scale_vec": scatter_about(seeds[4], (D,), 0.3, 2.5, (), jnp.float32),
        "gate_vec": scatter_about(seeds[5], (D,), 1.0, 4.0, ((0, 4),), jnp.float32),
        "qkv_weight": scatter_about(seeds[6], (D, 3 * HEADS * HD), D ** -0.5, 0.109375, ((0, 64), (1, 4))),
        "query_gain": jnp.clip(jnp.exp(jax.random.uniform(seeds[7], (HD,), jnp.float32, math.log(1.5), math.log(3.0))), 1.5, 3.0),
        "key_gain": jnp.clip(jnp.exp(jax.random.uniform(seeds[8], (HD,), jnp.float32, math.log(1.5), math.log(3.0))), 1.5, 3.0),
        "out_weight": scatter_about(seeds[9], (HEADS * HD, D), (HEADS * HD) ** -0.5, 0.15625, ((0, 4), (1, 64))),
    }


def modulate(source, shift_vec, scale_vec):
    values = source.astype(jnp.float32)
    center = lax.optimization_barrier(jnp.mean(values, axis=-1, keepdims=True))
    spread = lax.optimization_barrier(jnp.mean(jnp.square(values - center), axis=-1, keepdims=True))
    normed = (values - center) / jnp.sqrt(spread + 1e-06)
    return (normed * (1.0 + scale_vec) + shift_vec).astype(jnp.bfloat16)

def head_norm(values, gain):
    power = lax.optimization_barrier(jnp.mean(jnp.square(values), axis=-1, keepdims=True))
    return (values / jnp.sqrt(power + 1e-06) * gain).astype(jnp.bfloat16)

def reference(tokens, prompt, prompt_mask, shift_vec, scale_vec, gate_vec, qkv_weight, query_gain, key_gain, out_weight):
    inputs = jnp.concatenate([modulate(tokens, shift_vec, scale_vec), modulate(prompt, shift_vec, scale_vec)], axis=0)
    project = jnp.dot(inputs, qkv_weight, preferred_element_type=jnp.float32).reshape(inputs.shape[0], HEADS, 3, HD)
    queries = head_norm(project[:TOKENS, :, 0], query_gain)
    keys_all = head_norm(project[:, :, 1], key_gain)
    values_all = project[:, :, 2].astype(jnp.bfloat16)
    key_weight = jnp.concatenate([jnp.ones((TOKENS,), jnp.float32), prompt_mask.astype(jnp.float32)])
    inverse = 1.0 / math.sqrt(HD)
    block = math.gcd(TOKENS, 512)

    def attend_block(query_block):
        scores = jnp.einsum('qhd,khd->hqk', query_block.astype(jnp.float32), keys_all.astype(jnp.float32)) * inverse
        expon = jnp.exp(scores) * key_weight
        denom = lax.optimization_barrier(jnp.sum(expon, axis=-1))
        probs = lax.optimization_barrier(expon.astype(jnp.bfloat16))
        numer = jnp.einsum('hqk,khd->qhd', probs.astype(jnp.float32), values_all.astype(jnp.float32))
        return (numer / jnp.transpose(denom)[:, :, None]).astype(jnp.bfloat16)
    attended = lax.map(attend_block, queries.reshape(TOKENS // block, block, HEADS, HD)).reshape(TOKENS, HEADS * HD)
    mixed = jnp.dot(attended, out_weight, preferred_element_type=jnp.float32)
    return (mixed * gate_vec).astype(jnp.bfloat16)
```

```python
import functools
import math

import jax
import jax.numpy as jnp
from jax import lax
from jax.experimental import pallas as pl
from jax.experimental.pallas import tpu as pltpu
from jax.sharding import PartitionSpec as P

AX = ("seq", "head")
BF = jnp.bfloat16
F32 = jnp.float32
NT = (((1,), (1,)), ((), ()))
EXP2_SCALE = math.log2(math.e) / math.sqrt(128.0)
VMEM = 48 << 20
ANY = pl.BlockSpec(memory_space=pl.ANY)
SMEM = pl.BlockSpec(memory_space=pltpu.SMEM)
FULL = pl.BlockSpec(memory_space=pltpu.VMEM)


def place(device):
    seq, head = divmod(device, 4)
    return seq // 16, (seq // 4) % 4, (seq % 4) * 2 + head // 2, head % 2


def device_at(y, x, z, core):
    y, x, z = y % 4, x % 4, z % 8
    return (y * 16 + x * 4 + z // 2) * 4 + (z % 2) * 2 + core


def send(value, target):
    pairs = [(d, device_at(*target(*place(d)))) for d in range(256)]
    return lax.ppermute(value, AX, pairs)


def to_sibling(value):
    return send(value, lambda y, x, z, c: (y, x, z, 1 - c))


def round_z(value):
    return send(value, lambda y, x, z, c: (y, x, z + 1 - 2 * c, c))


def chip_blocks(kind, step, core):
    if kind == "own":
        return [("t", f ^ core) for f in (0, 1)]
    if step == 4:
        return [(f"r4" if f == core else "s4", None) for f in (0, 1)]
    mine = kind == "r"
    return [(f"{kind}{step}", f ^ core if mine else f ^ core ^ 1) for f in (0, 1)]


def pair_blocks(pair, z_lo, core):
    partner = "r" if z_lo != core else "s"
    other = "s" if z_lo != core else "r"
    first, second = {
        0: (("own", 0), (partner, 1)),
        1: ((other, 2), (other, 1)),
        2: ((partner, 2), (partner, 3)),
        3: (("own4", 4), (other, 3)),
    }[pair]
    if z_lo == 1:
        first, second = second, first
    return chip_blocks(*first, core) + chip_blocks(*second, core)


def modulate_rows(rows, load, shift_ref, gain_ref, out_ref):
    step = 16

    @pl.loop(0, rows // step)
    def _(i):
        at = pl.ds(pl.multiple_of(i * step, step), step)
        values = [load(at, b) for b in range(4)]
        center = sum(jnp.sum(v, axis=1, keepdims=True) for v in values) * (1.0 / 3072)
        values = [v - center for v in values]
        spread = sum(jnp.sum(v * v, axis=1, keepdims=True) for v in values) * (1.0 / 3072)
        scale = lax.rsqrt(spread + 1e-06)
        for b, v in enumerate(values):
            cols = slice(b * 768, (b + 1) * 768)
            out_ref[at, cols] = (v * scale * gain_ref[:, cols] + shift_ref[:, cols]).astype(BF)


def modulate_pair(pair, sources, flags, shift, gain):
    names = sorted(sources)

    def kernel(flags_ref, shift_ref, gain_ref, *refs):
        source = dict(zip(names, refs[: len(names)]))
        out_ref, buf, sems = refs[len(names) :]
        for z_lo in (0, 1):
            for core in (0, 1):

                @pl.when((flags_ref[0] == z_lo) & (flags_ref[1] == core))
                def _():
                    copies = []
                    for b, (name, index) in enumerate(pair_blocks(pair, z_lo, core)):
                        src = source[name] if index is None else source[name].at[index]
                        copies.append(pltpu.make_async_copy(src, buf.at[b], sems.at[b]))
                    for copy in copies:
                        copy.start()
                    for copy in copies:
                        copy.wait()

        modulate_rows(192, lambda at, b: buf[b, at, :].astype(F32), shift_ref, gain_ref, out_ref)

    return pl.pallas_call(
        kernel,
        out_shape=jax.ShapeDtypeStruct((192, 3072), BF),
        in_specs=[SMEM, FULL, FULL] + [ANY] * len(names),
        out_specs=FULL,
        scratch_shapes=[pltpu.VMEM((4, 192, 768), BF), pltpu.SemaphoreType.DMA((4,))],
        compiler_params=pltpu.CompilerParams(vmem_limit_bytes=VMEM),
        name=f"modulate{pair}",
    )(flags, shift, gain, *[sources[n] for n in names])


def modulate_prompt(prompt, flags, shift, gain):
    def kernel(flags_ref, shift_ref, gain_ref, prompt_ref, out_ref, buf, sem):
        at = pl.multiple_of(flags_ref[2] * 64, 64)
        copy = pltpu.make_async_copy(prompt_ref.at[pl.ds(at, 64), :], buf, sem)
        copy.start()
        copy.wait()
        load = lambda rows, b: buf[rows, b * 768 : (b + 1) * 768].astype(F32)
        modulate_rows(64, load, shift_ref, gain_ref, out_ref)

    return pl.pallas_call(
        kernel,
        out_shape=jax.ShapeDtypeStruct((64, 3072), BF),
        in_specs=[SMEM, FULL, FULL, ANY],
        out_specs=FULL,
        scratch_shapes=[pltpu.VMEM((64, 3072), BF), pltpu.SemaphoreType.DMA],
        compiler_params=pltpu.CompilerParams(vmem_limit_bytes=VMEM),
        name="modulate_prompt",
    )(flags, shift, gain, prompt)


def head_norm(values, gain):
    power = jnp.mean(values * values, axis=1, keepdims=True)
    return (values * lax.rsqrt(power + 1e-06) * gain).astype(BF)


def project(flags, inputs, prompt_inputs, weight_pieces, query_gain, key_gain):
    def kernel(flags_ref, qg_ref, kg_ref, x0, x1, x2, x3, xp, w0, w1, w2, w3, q_ref, k_ref, vt_ref, pk_ref, pvt_ref, w, x, px, v, sem_w, sem_x):
        core, y, x_at = flags_ref[1], flags_ref[2], flags_ref[3]
        copies = []
        for outer, piece in enumerate((w0, w1, w2, w3)):
            for inner in range(4):
                dx = jnp.where(core == 0, inner, outer)
                dy = jnp.where(core == 0, outer, inner)
                block = ((y + 4 - dy) % 4) * 4 + (x_at + 4 - dx) % 4
                dst = w.at[pl.ds(pl.multiple_of(block * 192, 192), 192), :]
                copies.append(pltpu.make_async_copy(piece.at[pl.ds(inner * 192, 192), :], dst, sem_w.at[outer * 4 + inner]))
        rows = [pltpu.make_async_copy(r, x.at[i], sem_x.at[i]) for i, r in enumerate((x0, x1, x2, x3))]
        rows.append(pltpu.make_async_copy(xp, px, sem_x.at[4]))
        for copy in copies + rows:
            copy.start()
        for copy in copies:
            copy.wait()
        for i in range(4):
            rows[i].wait()
            part = jnp.dot(x[i], w[...], preferred_element_type=F32)
            at = slice(i * 192, (i + 1) * 192)
            q_ref[at, :] = head_norm(part[:, :128], qg_ref[...])
            k_ref[at, :] = head_norm(part[:, 128:256], kg_ref[...])
            v[at, :] = part[:, 256:]
        vt_ref[...] = jnp.transpose(v[...]).astype(BF)
        rows[4].wait()
        part = jnp.dot(px[...], w[:, 128:], preferred_element_type=F32)
        pk_ref[...] = head_norm(part[:, :128], kg_ref[...])
        v[:64, :] = part[:, 128:]
        pvt_ref[...] = jnp.transpose(v[:128, :])[:, :64].astype(BF)

    shape = jax.ShapeDtypeStruct
    return pl.pallas_call(
        kernel,
        out_shape=(shape((768, 128), BF), shape((768, 128), BF), shape((128, 768), BF), shape((64, 128), BF), shape((128, 64), BF)),
        in_specs=[SMEM, FULL, FULL] + [ANY] * 9,
        out_specs=(FULL,) * 5,
        scratch_shapes=[
            pltpu.VMEM((3072, 384), BF),
            pltpu.VMEM((4, 192, 3072), BF),
            pltpu.VMEM((64, 3072), BF),
            pltpu.VMEM((768, 128), F32),
            pltpu.SemaphoreType.DMA((16,)),
            pltpu.SemaphoreType.DMA((5,)),
        ],
        compiler_params=pltpu.CompilerParams(vmem_limit_bytes=VMEM),
        name="project",
    )(flags, query_gain, key_gain, *inputs, prompt_inputs, *weight_pieces)


def attend(q, keys, values, prompt_key, prompt_value, prompt_weight):
    tile = 256

    def kernel(q_ref, k0, k1, k2, k3, v0, v1, v2, v3, pk, pv, pw, out_ref):
        for t in range(768 // tile):
            at = slice(t * tile, (t + 1) * tile)
            query = q_ref[at, :]
            scores = lax.dot_general(pk[...], query, NT, preferred_element_type=F32)
            expon = jnp.exp2(scores * EXP2_SCALE) * pw[:, :1]
            denom = jnp.sum(expon.reshape(8, 8, tile), axis=0)
            numer = jnp.dot(pv[...], expon.astype(BF), preferred_element_type=F32)
            for k_ref, v_ref in ((k0, v0), (k1, v1), (k2, v2), (k3, v3)):
                scores = lax.dot_general(k_ref[...], query, NT, preferred_element_type=F32)
                expon = jnp.exp2(scores * EXP2_SCALE)
                denom = denom + jnp.sum(expon.reshape(96, 8, tile), axis=0)
                numer = numer + jnp.dot(v_ref[...], expon.astype(BF), preferred_element_type=F32)
            total = jnp.sum(denom, axis=0, keepdims=True)
            high = total.astype(BF).astype(F32)
            out_ref[0:128, at] = numer.astype(BF)
            out_ref[128:144, at] = jnp.concatenate([high, total - high, jnp.zeros((14, tile), F32)], axis=0).astype(BF)

    return pl.pallas_call(
        kernel,
        out_shape=jax.ShapeDtypeStruct((144, 768), BF),
        in_specs=[FULL] * 12,
        out_specs=FULL,
        compiler_params=pltpu.CompilerParams(vmem_limit_bytes=VMEM),
        cost_estimate=pl.CostEstimate(flops=4 * 128 * 768 * 3136, bytes_accessed=2 << 20, transcendentals=768 * 3136),
        name="attend",
    )(q, *keys, *values, prompt_key, prompt_value, prompt_weight)


def combine(parts):
    def kernel(a, b, c, d, out_ref):
        parts = [r[...].astype(F32) for r in (a, b, c, d)]
        total = parts[0] + parts[1] + parts[2] + parts[3]
        denom = total[128:129, :] + total[129:130, :]
        out_ref[...] = jnp.transpose(total[:128, :] / denom).astype(BF)

    return pl.pallas_call(
        kernel,
        out_shape=jax.ShapeDtypeStruct((768, 128), BF),
        in_specs=[FULL] * 4,
        out_specs=FULL,
        compiler_params=pltpu.CompilerParams(vmem_limit_bytes=VMEM),
        name="combine",
    )(*parts)


def project_out(flags, gathered, weight, gate):
    def kernel(flags_ref, near, far, weight_ref, gate_ref, out_ref, rows):
        z_lo, core, z_hi = flags_ref[0], flags_ref[1], flags_ref[4]
        for i in range(16):
            cross, other, r = i // 8, (i // 4) % 2, i % 4
            low = jnp.where(other == 0, z_lo, 1 - z_lo)
            head_group = low * 2 + jnp.where(cross == 0, core, 1 - core)
            turn = {0: 0, 1: 1 - 2 * low, 2: 2 * low - 1, 3: 2}[r]
            member = (z_hi + 4 + turn) % 4
            src = near if cross == 0 else far

            @pl.when(member < 3)
            def _():
                at = pl.multiple_of(head_group * 384 + member * 128, 128)
                start = (i % 8) * 192
                rows[:, pl.ds(at, 128)] = src[start : start + 192, :]

        total = jnp.zeros((192, 768), F32)
        for h in range(4):
            total = total + lax.dot_general(rows[:, h * 384 : (h + 1) * 384], weight_ref[h], NT, preferred_element_type=F32)
        out_ref[...] = (total * gate_ref[...]).astype(BF)

    return pl.pallas_call(
        kernel,
        out_shape=jax.ShapeDtypeStruct((192, 768), BF),
        in_specs=[SMEM] + [FULL] * 4,
        out_specs=FULL,
        scratch_shapes=[pltpu.VMEM((192, 1536), BF)],
        compiler_params=pltpu.CompilerParams(vmem_limit_bytes=VMEM),
        name="project_out",
    )(flags, *gathered, weight, gate)


def body(tokens, prompt, prompt_mask, shift_vec, scale_vec, gate_vec, qkv_weight, query_gain, key_gain, out_weight):
    seq, head = lax.axis_index("seq"), lax.axis_index("head")
    y, x, z_hi, z_lo, core = seq // 16, (seq // 4) % 4, seq % 4, head // 2, head % 2
    flags = jnp.stack([z_lo, core, y, x, z_hi]).astype(jnp.int32)
    shift, gain = shift_vec[None], 1.0 + scale_vec[None]

    def columns(member):
        return lax.dynamic_slice(qkv_weight, (0, 384 * jnp.minimum(member, 2)), (48, 384))

    own = columns(z_hi)
    moved = [send(columns((z_hi + k) % 4), lambda y, x, z, c, k=k: (y, x, z + 2 * k, c)) for k in (1, 2, 3)]
    cycle = [moved[2], moved[1], moved[0], own]
    own_rows = lax.dynamic_slice(jnp.concatenate(cycle + cycle, axis=0), (48 * (3 - z_hi), 0), (192, 384))

    sources = {"t": jnp.stack([tokens, to_sibling(tokens)])}
    moving = sources["t"]
    for step in (1, 2, 3):
        moving = sources[f"r{step}"] = round_z(moving)
    sources["r4"] = round_z(moving[0])
    for step in (1, 2, 3, 4):
        sources[f"s{step}"] = to_sibling(sources[f"r{step}"])

    def used(pair):
        names = {n for z in (0, 1) for c in (0, 1) for n, _ in pair_blocks(pair, z, c)}
        return {n: sources[n] for n in names}

    def first(k):
        return lambda y, x, z, c: (y, x + k, z, c) if c == 0 else (y + k, x, z, c)

    def second(k):
        return lambda y, x, z, c: (y + k, x, z, c) if c == 0 else (y, x + k, z, c)

    line = jnp.concatenate([own_rows] + [send(own_rows, first(k)) for k in (1, 2, 3)], axis=0)
    pieces = [line] + [send(line, second(k)) for k in (1, 2, 3)]

    turned = jnp.transpose(out_weight)
    swap = [((d // 64 * 16 + d // 4 % 16) * 4 + d % 4, (d % 4 * 16 + d // 4 % 16) * 4 + d // 64) for d in range(256)]
    turned = lax.ppermute(turned, AX, swap)
    out_columns = lax.all_gather(turned, "seq", axis=0, tiled=True).reshape(4, 768, 384)

    inputs = [modulate_pair(pair, used(pair), flags, shift, gain) for pair in range(4)]
    prompt_inputs = modulate_prompt(prompt, flags, shift, gain)
    q, k, vt, pk, pvt = project(flags, inputs, prompt_inputs, pieces, query_gain[None], key_gain[None])

    queries = [q] + [send(q, lambda y, x, z, c, n=n: (y + n, x, z, c)) for n in (1, 2, 3)]
    keys = [k] + [send(k, lambda y, x, z, c, n=n: (y, x + n, z, c)) for n in (1, 2, 3)]
    values = [vt] + [send(vt, lambda y, x, z, c, n=n: (y, x + n, z, c)) for n in (1, 2, 3)]
    weight = lax.dynamic_slice(prompt_mask, (64 * y,), (64,)).astype(F32)
    weight = jnp.broadcast_to(weight[:, None], (64, 128))
    parts = [attend(part, keys, values, pk, pvt, weight) for part in queries]
    parts = [parts[0]] + [send(parts[n], lambda y, x, z, c, n=n: (y - n, x, z, c)) for n in (1, 2, 3)]
    attended = combine(parts)

    def turn(n):
        step = {1: lambda low: -1 + 2 * low, 2: lambda low: 1 - 2 * low, 3: lambda low: 2}[n]
        return lambda y, x, z, c: (y, x, z + 2 * step(z % 2), c)

    blocks = [attended[:192]] + [send(attended[192 * n : 192 * (n + 1)], turn(n)) for n in (1, 2, 3)]
    blocks = jnp.concatenate(blocks, axis=0)
    across = send(blocks, lambda y, x, z, c: (y, x, z ^ 1, c))
    near = jnp.concatenate([blocks, across], axis=0)
    far = to_sibling(near)
    return project_out(flags, (near, far), out_columns, gate_vec[None])


def solution(mesh):
    placed = (P("seq", "head"), P(), P(), P(), P(), P("head"), P("seq", "head"), P(), P(), P("head", "seq"))
    return jax.shard_map(body, mesh=mesh, in_specs=placed, out_specs=P("seq", "head"), check_vma=False)
```

```python
import math

import jax
import jax.numpy as jnp
from jax import lax
from jax.experimental import pallas as pl
from jax.experimental.pallas import tpu as pltpu
from jax.sharding import PartitionSpec as P

AX = ("seq", "head")
ORDER = (0, 1, 3, 2)
BF = jnp.bfloat16
F32 = jnp.float32
NT = (((1,), (1,)), ((), ()))
EXP2_SCALE = math.log2(math.e) / math.sqrt(128.0)
VMEM = 48 << 20
ANY = pl.BlockSpec(memory_space=pl.ANY)
SMEM = pl.BlockSpec(memory_space=pltpu.SMEM)
FULL = pl.BlockSpec(memory_space=pltpu.VMEM)


def place(device):
    seq, head = divmod(device, 4)
    return seq // 16, (seq // 4) % 4, (seq % 4) * 2 + head // 2, head % 2


def device_at(y, x, z, core):
    y, x, z = y % 4, x % 4, z % 8
    return (y * 16 + x * 4 + z // 2) * 4 + (z % 2) * 2 + core


def send(value, target):
    pairs = [(d, device_at(*target(*place(d)))) for d in range(256)]
    return lax.ppermute(value, AX, pairs)


def to_sibling(value):
    return send(value, lambda y, x, z, c: (y, x, z, 1 - c))


def round_z(value):
    return send(value, lambda y, x, z, c: (y, x, z + 1 - 2 * c, c))


def cost(microseconds):
    return pl.CostEstimate(flops=0, bytes_accessed=int(microseconds * 3e6), transcendentals=0)


def params():
    return pltpu.CompilerParams(vmem_limit_bytes=VMEM)


def own_blocks(sources, z_lo, core):
    near = z_lo != core
    first, second = sources[:2] if near else sources[2:]
    if (z_lo == 1) == near:
        first, second = second, first
    return [(chip, (f ^ core) * 192) for chip in (first, second) for f in (0, 1)]


def last_blocks(z_lo, core):
    far = z_lo == core
    third = [(0, (f ^ core) * 192) if far else (1, (f ^ core ^ 1) * 192) for f in (0, 1)]
    fourth = [(2 if f == core else 3, 0) for f in (0, 1)]
    return fourth + third if z_lo == 0 else third + fourth


def modulate_rows(rows, step, load, shift_ref, gain_ref, out_ref):
    @pl.loop(0, rows // step)
    def _(i):
        at = pl.ds(pl.multiple_of(i * step, step), step)
        total = jnp.zeros((step, 128), F32)
        for b in range(24):
            total = total + load(at, b)
        center = jnp.sum(total, axis=1, keepdims=True) * (1.0 / 3072)
        total = jnp.zeros((step, 128), F32)
        for b in range(24):
            value = load(at, b) - center
            total = total + value * value
        scale = lax.rsqrt(jnp.sum(total, axis=1, keepdims=True) * (1.0 / 3072) + 1e-06)
        for b in range(24):
            cols = slice(b * 128, (b + 1) * 128)
            out_ref[at, cols] = ((load(at, b) - center) * scale * gain_ref[:, cols] + shift_ref[:, cols]).astype(BF)


def modulate_block(sources, choose, flags, shift, gain):
    count = len(sources)

    def kernel(flags_ref, shift_ref, gain_ref, *refs):
        out_ref = refs[count]
        for z_lo in (0, 1):
            for core in (0, 1):

                @pl.when((flags_ref[0] == z_lo) & (flags_ref[1] == core))
                def _():
                    blocks = choose(z_lo, core)

                    def load(at, b):
                        source, start = blocks[b // 6]
                        cols = slice(b % 6 * 128, (b % 6 + 1) * 128)
                        return refs[source][pl.ds(pl.multiple_of(start + at.start, 64), at.size), cols].astype(F32)

                    modulate_rows(192, 64, load, shift_ref, gain_ref, out_ref)

    return pl.pallas_call(
        kernel,
        out_shape=jax.ShapeDtypeStruct((192, 3072), BF),
        in_specs=[SMEM, FULL, FULL] + [FULL] * count,
        out_specs=FULL,
        compiler_params=params(),
        cost_estimate=cost(2.5),
        name="modulate",
    )(flags, shift, gain, *sources)


def modulate_prompt(prompt, flags, shift, gain):
    def kernel(flags_ref, shift_ref, gain_ref, prompt_ref, out_ref, buf, sem):
        at = pl.multiple_of(flags_ref[2] * 64, 64)
        copy = pltpu.make_async_copy(prompt_ref.at[pl.ds(at, 64), :], buf, sem)
        copy.start()
        copy.wait()
        load = lambda rows, b: buf[rows, b * 128 : (b + 1) * 128].astype(F32)
        modulate_rows(64, 64, load, shift_ref, gain_ref, out_ref)

    return pl.pallas_call(
        kernel,
        out_shape=jax.ShapeDtypeStruct((64, 3072), BF),
        in_specs=[SMEM, FULL, FULL, ANY],
        out_specs=FULL,
        scratch_shapes=[pltpu.VMEM((64, 3072), BF), pltpu.SemaphoreType.DMA],
        compiler_params=params(),
        cost_estimate=cost(1.5),
        name="modulate_prompt",
    )(flags, shift, gain, prompt)


def head_norm(values, gain):
    power = jnp.mean(values * values, axis=1, keepdims=True)
    return (values * lax.rsqrt(power + 1e-06) * gain).astype(BF)


def gathered_blocks(flags_ref, pieces):
    core, y, x = flags_ref[1], flags_ref[2], flags_ref[3]
    for outer, piece in enumerate(pieces):
        for inner in range(4):
            dx = jnp.where(core == 0, ORDER[inner], ORDER[outer])
            dy = jnp.where(core == 0, ORDER[outer], ORDER[inner])
            block = ((y + 4 - dy) % 4) * 4 + (x + 4 - dx) % 4
            yield block, piece[inner * 192 : (inner + 1) * 192, :]


def project(flags, inputs, prompt_inputs, weight_pieces, query_gain, key_gain):
    def kernel(flags_ref, qg_ref, kg_ref, x0, x1, x2, x3, x4, xp, w0, w1, w2, w3, q_ref, kv_ref, pk_ref, pvt_ref, w, part):
        for block, source in gathered_blocks(flags_ref, (w0, w1, w2, w3)):
            w[pl.ds(pl.multiple_of(block * 192, 192), 192), :] = source
        near = flags_ref[0] != flags_ref[1]
        for i, rows in enumerate((x0, x1)):
            at = pl.ds(pl.multiple_of(jnp.where(near, i, 1 - i) * 192, 192), 192)
            part[at, :] = jnp.dot(rows[...], w[...], preferred_element_type=F32)
        for mine, rows in ((True, x2), (False, x3)):

            @pl.when(near == mine)
            def _():
                part[384:576, :] = jnp.dot(rows[...], w[...], preferred_element_type=F32)

        part[576:768, :] = jnp.dot(x4[...], w[...], preferred_element_type=F32)
        part[768:832, :] = jnp.dot(xp[...], w[...], preferred_element_type=F32)
        part[832:896, :] = jnp.zeros((64, 384), F32)
        for i in range(6):
            at = slice(i * 128, (i + 1) * 128)
            q_ref[at, :] = head_norm(part[at, :128], qg_ref[...])
            kv_ref[at, :] = head_norm(part[at, 128:256], kg_ref[...])
            kv_ref[768 + i * 128 : 896 + i * 128, :] = jnp.transpose(part[at, 256:]).astype(BF)
        pk_ref[...] = head_norm(part[768:832, 128:256], kg_ref[...])
        pvt_ref[...] = jnp.transpose(part[768:896, 256:])[:, :64].astype(BF)

    shape = jax.ShapeDtypeStruct
    return pl.pallas_call(
        kernel,
        out_shape=(shape((768, 128), BF), shape((1536, 128), BF), shape((64, 128), BF), shape((128, 64), BF)),
        in_specs=[SMEM] + [FULL] * 12,
        out_specs=(FULL,) * 4,
        scratch_shapes=[pltpu.VMEM((3072, 384), BF), pltpu.VMEM((896, 384), F32)],
        compiler_params=params(),
        cost_estimate=cost(6),
        name="project",
    )(flags, query_gain, key_gain, *inputs, prompt_inputs, *weight_pieces)


def attend(queries, pairs, prompt, sums, last):
    tile = 256
    n, m = len(queries), len(pairs)

    def kernel(*refs):
        refs = list(refs)
        q_refs, rest = refs[:n], refs[n:]
        kv_refs = []
        for pair in pairs:
            kv_refs.append((rest[0], rest[len(pair) - 1], 768 * (len(pair) == 1)))
            rest = rest[len(pair) :]
        if prompt:
            pk, pv, pw = rest[:3]
            rest = rest[3:]
        sum_refs = rest[: len(sums)]
        out_refs = rest[len(sums) :]
        for i in range(n):
            for t in range(768 // tile):
                at = slice(t * tile, (t + 1) * tile)
                query = q_refs[i][at, :]
                if sums:
                    numer, denom = sum_refs[i][0:128, at], sum_refs[i][128:136, at]
                else:
                    numer, denom = jnp.zeros((128, tile), F32), jnp.zeros((8, tile), F32)
                for keys, values, start in kv_refs:
                    scores = lax.dot_general(keys[0:768, :], query, NT, preferred_element_type=F32)
                    expon = jnp.exp2(scores * EXP2_SCALE)
                    denom = denom + jnp.sum(expon.reshape(96, 8, tile), axis=0)
                    value = jnp.concatenate([values[start + 128 * j : start + 128 * (j + 1), :] for j in range(6)], axis=1)
                    numer = numer + jnp.dot(value, expon.astype(BF), preferred_element_type=F32)
                if prompt:
                    scores = lax.dot_general(pk[...], query, NT, preferred_element_type=F32)
                    expon = jnp.exp2(scores * EXP2_SCALE) * pw[:, :1]
                    denom = denom + jnp.sum(expon.reshape(8, 8, tile), axis=0)
                    numer = numer + jnp.dot(pv[...], expon.astype(BF), preferred_element_type=F32)
                if last:
                    total = jnp.sum(denom, axis=0, keepdims=True)
                    high = total.astype(BF).astype(F32)
                    out_refs[i][0:128, at] = numer.astype(BF)
                    low = jnp.concatenate([high, total - high, jnp.zeros((14, tile), F32)], axis=0)
                    out_refs[i][128:144, at] = low.astype(BF)
                else:
                    out_refs[i][0:128, at] = numer
                    out_refs[i][128:136, at] = denom

    out = jax.ShapeDtypeStruct((144, 768), BF) if last else jax.ShapeDtypeStruct((136, 768), F32)
    args = [*queries, *[part for pair in pairs for part in pair], *prompt, *sums]
    return pl.pallas_call(
        kernel,
        out_shape=(out,) * n,
        in_specs=[FULL] * len(args),
        out_specs=(FULL,) * n,
        compiler_params=params(),
        cost_estimate=cost(0.7 * n * m),
        name="attend",
    )(*args)


def combine(parts):
    def kernel(a, b, c, d, *out_refs):
        parts = [r[...].astype(F32) for r in (a, b, c, d)]
        total = parts[0] + parts[1] + parts[2] + parts[3]
        denom = total[128:129, :] + total[129:130, :]
        rows = jnp.transpose(total[:128, :] / denom).astype(BF)
        for i, out_ref in enumerate(out_refs):
            out_ref[...] = rows[192 * i : 192 * (i + 1), :]

    return pl.pallas_call(
        kernel,
        out_shape=(jax.ShapeDtypeStruct((192, 128), BF),) * 4,
        in_specs=[FULL] * 4,
        out_specs=(FULL,) * 4,
        compiler_params=params(),
        cost_estimate=cost(0.5),
        name="combine",
    )(*parts)


def project_out(flags, gathered, weight_pieces, gate):
    def kernel(flags_ref, near0, near1, near2, near3, across, far, far_across, w0, w1, w2, w3, gate_ref, out_ref, rows, weight):
        z_lo, core, z_hi = flags_ref[0], flags_ref[1], flags_ref[4]
        for block, source in gathered_blocks(flags_ref, (w0, w1, w2, w3)):
            weight[block // 4, pl.ds(pl.multiple_of(block % 4 * 192, 192), 192), :] = source
        for i in range(16):
            cross, other, r = i // 8, (i // 4) % 2, i % 4
            low = jnp.where(other == 0, z_lo, 1 - z_lo)
            head_group = low * 2 + jnp.where(cross == 0, core, 1 - core)
            turn = {0: 0, 1: 1 - 2 * low, 2: 2 * low - 1, 3: 2}[r]
            member = (z_hi + 4 + turn) % 4
            if i < 4:
                src, start = (near0, near1, near2, near3)[i], 0
            else:
                src, start = (None, across, far, far_across)[i // 4], r * 192

            @pl.when(member < 3)
            def _():
                at = pl.multiple_of(head_group * 384 + member * 128, 128)
                rows[:, pl.ds(at, 128)] = src[start : start + 192, :]

        total = jnp.zeros((192, 768), F32)
        for h in range(4):
            total = total + lax.dot_general(rows[:, h * 384 : (h + 1) * 384], weight[h], NT, preferred_element_type=F32)
        out_ref[...] = (total * gate_ref[...]).astype(BF)

    return pl.pallas_call(
        kernel,
        out_shape=jax.ShapeDtypeStruct((192, 768), BF),
        in_specs=[SMEM] + [FULL] * 12,
        out_specs=FULL,
        scratch_shapes=[pltpu.VMEM((192, 1536), BF), pltpu.VMEM((4, 768, 384), BF)],
        compiler_params=params(),
        cost_estimate=cost(3),
        name="project_out",
    )(flags, *gathered, *weight_pieces, gate)


def head_columns(flags, weight, turned):
    def kernel(flags_ref, weight_ref, turned_ref, *out_refs):
        for k, out_ref in enumerate(out_refs):
            member = jnp.minimum((flags_ref[4] + k) % 4, 2)
            out_ref[0:48, :] = weight_ref[:, pl.ds(pl.multiple_of(member * 384, 128), 384)]
            out_ref[48:96, :] = turned_ref[...]

    return pl.pallas_call(
        kernel,
        out_shape=(jax.ShapeDtypeStruct((96, 384), BF),) * 4,
        in_specs=[SMEM, FULL, FULL],
        out_specs=(FULL,) * 4,
        compiler_params=params(),
        cost_estimate=cost(0.3),
        name="head_columns",
    )(flags, weight, turned)


def by_z_hi(flags, blocks):
    def kernel(flags_ref, b0, b1, b2, b3, out_ref):
        for k, block in enumerate((b0, b1, b2, b3)):
            at = pl.multiple_of((flags_ref[4] + 4 - k) % 4 * 48, 16)
            out_ref[pl.ds(at, 48), :] = block[0:48, :]
            out_ref[pl.ds(192 + at, 48), :] = block[48:96, :]

    return pl.pallas_call(
        kernel,
        out_shape=jax.ShapeDtypeStruct((384, 384), BF),
        in_specs=[SMEM] + [FULL] * 4,
        out_specs=FULL,
        compiler_params=params(),
        cost_estimate=cost(0.3),
        name="by_z_hi",
    )(flags, *blocks)


def lines(arrays):
    def kernel(*refs):
        for i, ref in enumerate(refs[:4]):
            refs[4][i * 192 : (i + 1) * 192, :] = ref[0:192, :]
            refs[5][i * 192 : (i + 1) * 192, :] = ref[192:384, :]

    return pl.pallas_call(
        kernel,
        out_shape=(jax.ShapeDtypeStruct((768, 384), BF),) * 2,
        in_specs=[FULL] * 4,
        out_specs=(FULL,) * 2,
        compiler_params=params(),
        cost_estimate=cost(0.4),
        name="lines",
    )(*arrays)


def over(arrays):
    rows, width = arrays[0].shape

    def kernel(*refs):
        for i, ref in enumerate(refs[:-1]):
            refs[-1][i * rows : (i + 1) * rows, :] = ref[...]

    return pl.pallas_call(
        kernel,
        out_shape=jax.ShapeDtypeStruct((len(arrays) * rows, width), arrays[0].dtype),
        in_specs=[FULL] * len(arrays),
        out_specs=FULL,
        compiler_params=params(),
        cost_estimate=cost(0.4),
        name="over",
    )(*arrays)


def after(value, *others):
    return lax.optimization_barrier((value, *others))[0]


def together(*values):
    return lax.optimization_barrier(values)


def body(tokens, prompt, prompt_mask, shift_vec, scale_vec, gate_vec, qkv_weight, query_gain, key_gain, out_weight):
    seq, head = lax.axis_index("seq"), lax.axis_index("head")
    y, x, z_hi, z_lo, core = seq // 16, (seq // 4) % 4, seq % 4, head // 2, head % 2
    flags = jnp.stack([z_lo, core, y, x, z_hi]).astype(jnp.int32)
    shift, gain = shift_vec[None], 1.0 + scale_vec[None]
    prompt_weight = lax.dynamic_slice(prompt_mask, (64 * y,), (64,)).astype(F32)
    prompt_weight = jnp.broadcast_to(prompt_weight[:, None], (64, 128))

    swap = [(d, device_at(d % 4, x, z // 2 * 2 + y // 2, y % 2)) for d in range(256) for y, x, z, c in [place(d)]]
    turned = lax.ppermute(jnp.transpose(out_weight), AX, swap)
    tokens, sibling, turned = together(tokens, to_sibling(tokens), turned)
    own = over([tokens, sibling])

    rows = head_columns(flags, qkv_weight, turned)
    rows = [rows[0]] + [send(rows[k], lambda y, x, z, c: (y, x, z + 2 * k, c)) for k in (1, 3, 2)]
    rows = [rows[0], rows[1], rows[3], rows[2]]
    ring1, *rows = together(round_z(own), *rows)
    column = by_z_hi(flags, rows)

    def along(k, core_x):
        return lambda y, x, z, c: (y, x + k, z, c) if c == core_x else (y + k, x, z, c)

    ring2, prompt_weight, *line = together(round_z(ring1), prompt_weight, column, *[send(column, along(k, 0)) for k in (1, 3, 2)])
    line, out_line = lines(line)
    weight1, weight3 = [send(line, along(k, 1)) for k in (1, 3)]
    rows1 = modulate_block((own, ring1, ring2), lambda z, c: own_blocks((0, 1, 1, 2), z, c), flags, shift, gain)
    ring3, rows1, weight1, weight3 = together(round_z(ring2), rows1, weight1, weight3)
    weight2 = send(after(line, weight1), along(2, 1))
    half = round_z(ring3[:192])
    rows2 = modulate_block((ring2, ring3), lambda z, c: own_blocks((0, 1, 0, 1), z, c), flags, shift, gain)
    half, sibling1, sibling3, sibling2 = together(half, to_sibling(rows1), to_sibling(ring3), to_sibling(rows2))
    rows3 = modulate_block((ring3, sibling3, half, to_sibling(half)), last_blocks, flags, shift, gain)
    inputs = [rows1, sibling1, rows2, sibling2, rows3]
    prompt_inputs = modulate_prompt(prompt, flags, shift, gain)
    weight_pieces = [line, weight1, weight3, weight2]
    out1, out3 = [send(after(out_line, weight2), along(k, 1)) for k in (1, 3)]
    q, kv, pk, pvt = project(flags, inputs, prompt_inputs, weight_pieces, query_gain[None], key_gain[None])
    out2 = send(after(out_line, q, out1), along(2, 1))
    out_pieces = [out_line, out1, out3, out2]

    kv1, kv3 = [send(kv, lambda y, x, z, c: (y, x + n, z, c)) for n in (1, 3)]
    q1, q3 = [send(q, lambda y, x, z, c: (y + n, x, z, c)) for n in (1, 3)]
    kv1, kv3, q1, q3 = together(kv1, kv3, q1, q3)
    kv2 = send(after(kv, kv1), lambda y, x, z, c: (y, x + 2, z, c))
    q2 = send(after(q, q1), lambda y, x, z, c: (y + 2, x, z, c))
    prompt_parts = (pk, pvt, prompt_weight)
    sums = attend((q1, q3, q), ((kv,), (kv1,), (kv3,)), prompt_parts, (), False)
    q2, *sums = together(q2, *sums)
    (part2,) = attend((q2,), ((kv,), (kv1,), (kv3,), (kv2,)), prompt_parts, (), True)
    part1, part3, part0 = attend((q1, q3, q), ((kv2,),), (), sums, True)
    parts = [part0] + [send(p, lambda y, x, z, c: (y - n, x, z, c)) for n, p in ((2, part2), (1, part1), (3, part3))]
    attended = combine(parts)

    def turn(n):
        step = {1: lambda low: -1 + 2 * low, 2: lambda low: 1 - 2 * low, 3: lambda low: 2}[n]
        return lambda y, x, z, c: (y, x, z + 2 * step(z % 2), c)

    near = [attended[0]] + [send(attended[n], turn(n)) for n in (1, 2, 3)]
    blocks = over(near)
    across = send(blocks, lambda y, x, z, c: (y, x, z ^ 1, c))
    gathered = (*near, across, to_sibling(blocks), to_sibling(across))
    return project_out(flags, gathered, out_pieces, gate_vec[None])


def solution(mesh):
    placed = (P("seq", "head"), P(), P(), P(), P(), P("head"), P("seq", "head"), P(), P(), P("head", "seq"))
    return jax.shard_map(body, mesh=mesh, in_specs=placed, out_specs=P("seq", "head"), check_vma=False)
```

```python
import math

import jax
import jax.numpy as jnp
from jax import lax
from jax.experimental import pallas as pl
from jax.experimental.pallas import tpu as pltpu
from jax.sharding import PartitionSpec as P

AX = ("seq", "head")
ORDER = (0, 1, 3, 2)
BF = jnp.bfloat16
F32 = jnp.float32
NT = (((1,), (1,)), ((), ()))
EXP2_SCALE = math.log2(math.e) / math.sqrt(128.0)
VMEM = 20 << 20
ANY = pl.BlockSpec(memory_space=pl.ANY)
SMEM = pl.BlockSpec(memory_space=pltpu.SMEM)
FULL = pl.BlockSpec(memory_space=pltpu.VMEM)
HBM = pl.BlockSpec(memory_space=pltpu.HBM)


def place(device):
    seq, head = divmod(device, 4)
    return seq // 16, (seq // 4) % 4, (seq % 4) * 2 + head // 2, head % 2


def device_at(y, x, z, core):
    y, x, z = y % 4, x % 4, z % 8
    return (y * 16 + x * 4 + z // 2) * 4 + (z % 2) * 2 + core


def send(value, target):
    pairs = [(d, device_at(*target(*place(d)))) for d in range(256)]
    return lax.ppermute(value, AX, pairs)


def to_sibling(value):
    return send(value, lambda y, x, z, c: (y, x, z, 1 - c))


def round_z(value):
    return send(value, lambda y, x, z, c: (y, x, z + 1 - 2 * c, c))


def cost(microseconds):
    return pl.CostEstimate(flops=0, bytes_accessed=int(microseconds * 3e6), transcendentals=0)


def params():
    return pltpu.CompilerParams(vmem_limit_bytes=VMEM)


def first_blocks(z_lo, core):
    near = z_lo != core
    first, second = (0, 1) if near else (1, 2)
    if (z_lo == 1) == near:
        first, second = second, first
    return [2 * chip + (f ^ core) for chip in (first, second) for f in (0, 1)]


def third_blocks(z_lo, core):
    if z_lo != core:
        chips = [[0 + (f ^ core), 2 + (f ^ core)] for f in (0, 1)]
    else:
        chips = [[(4, 192 * (f ^ core ^ 1)), (4, 192 * (2 + (f ^ core ^ 1)))] for f in (0, 1)]
    first, second = [chips[0][0], chips[1][0]], [chips[0][1], chips[1][1]]
    return first + second if z_lo == 0 else second + first


def last_blocks(z_lo, core):
    third = [f ^ core if z_lo == core else (3, 192 * (2 + (f ^ core ^ 1))) for f in (0, 1)]
    fourth = [2 if f == core else (3, 192 * 4) for f in (0, 1)]
    return fourth + third if z_lo == 0 else third + fourth


def modulate_rows(rows, step, load, shift_ref, gain_ref, out_ref):
    @pl.loop(0, rows // step)
    def _(i):
        at = pl.ds(pl.multiple_of(i * step, step), step)
        total = jnp.zeros((step, 128), F32)
        for b in range(24):
            total = total + load(at, b)
        center = jnp.sum(total, axis=1, keepdims=True) * (1.0 / 3072)
        total = jnp.zeros((step, 128), F32)
        for b in range(24):
            value = load(at, b) - center
            total = total + value * value
        scale = lax.rsqrt(jnp.sum(total, axis=1, keepdims=True) * (1.0 / 3072) + 1e-06)
        for b in range(24):
            cols = slice(b * 128, (b + 1) * 128)
            out_ref[at, cols] = ((load(at, b) - center) * scale * (1.0 + gain_ref[:, cols]) + shift_ref[:, cols]).astype(BF)


def modulate_block(sources, choose, flags, shift, gain, far_sources=0):
    count = len(sources)

    def kernel(flags_ref, shift_ref, gain_ref, *refs):
        out_ref, buf, sems = refs[count:]
        for z_lo in (0, 1):
            for core in (0, 1):

                @pl.when((flags_ref[0] == z_lo) & (flags_ref[1] == core))
                def _():
                    copies = []
                    for b, source in enumerate(choose(z_lo, core)):
                        source, start = source if isinstance(source, tuple) else (source, 0)
                        cols = slice(b * 768, (b + 1) * 768)
                        if source < far_sources:
                            copies.append(pltpu.make_async_copy(refs[source], buf.at[:, cols], sems.at[b]))
                            copies[-1].start()
                        else:
                            buf[:, cols] = refs[source][start : start + 192, :]
                    for copy in copies:
                        copy.wait()

        load = lambda at, b: buf[at, b * 128 : (b + 1) * 128].astype(F32)
        modulate_rows(192, 64, load, shift_ref, gain_ref, out_ref)

    return pl.pallas_call(
        kernel,
        out_shape=jax.ShapeDtypeStruct((192, 3072), BF),
        in_specs=[SMEM, FULL, FULL] + [HBM] * far_sources + [FULL] * (count - far_sources),
        out_specs=FULL,
        scratch_shapes=[pltpu.VMEM((192, 3072), BF), pltpu.SemaphoreType.DMA((4,))],
        compiler_params=params(),
        cost_estimate=cost(6),
        name="modulate",
    )(flags, shift, gain, *sources)


def modulate_prompt(prompt, flags, shift, gain):
    def kernel(flags_ref, shift_ref, gain_ref, prompt_ref, out_ref, buf, sem):
        at = pl.multiple_of(flags_ref[2] * 64, 64)
        copy = pltpu.make_async_copy(prompt_ref.at[pl.ds(at, 64), :], buf, sem)
        copy.start()
        copy.wait()
        load = lambda rows, b: buf[rows, b * 128 : (b + 1) * 128].astype(F32)
        modulate_rows(64, 64, load, shift_ref, gain_ref, out_ref)

    return pl.pallas_call(
        kernel,
        out_shape=jax.ShapeDtypeStruct((64, 3072), BF),
        in_specs=[SMEM, FULL, FULL, HBM],
        out_specs=FULL,
        scratch_shapes=[pltpu.VMEM((64, 3072), BF), pltpu.SemaphoreType.DMA],
        compiler_params=params(),
        cost_estimate=cost(6),
        name="modulate_prompt",
    )(flags, shift, gain, prompt)


def head_norm(values, gain):
    power = jnp.mean(values * values, axis=1, keepdims=True)
    return (values * lax.rsqrt(power + 1e-06) * gain).astype(BF)


def gathered_blocks(flags_ref, pieces, x_inside):
    core, y, x = flags_ref[1], flags_ref[2], flags_ref[3]
    for outer, piece in enumerate(pieces):
        for inner in range(4):
            dx = jnp.where(core == x_inside, ORDER[inner], ORDER[outer])
            dy = jnp.where(core == x_inside, ORDER[outer], ORDER[inner])
            block = ((y + 4 - dy) % 4) * 4 + (x + 4 - dx) % 4
            yield block, piece[inner * 192 : (inner + 1) * 192, :]


def project(flags, inputs, prompt_inputs, weight_pieces, query_gain, key_gain):
    def kernel(flags_ref, qg_ref, kg_ref, x0, x1, x2, x3, xp, w0, w1, w2, w3, q_ref, kv_ref, pk_ref, pvt_ref, w, part):
        for block, source in gathered_blocks(flags_ref, (w0, w1, w2, w3), 0):
            w[pl.ds(pl.multiple_of(block * 192, 192), 192), :] = source
        near = flags_ref[0] != flags_ref[1]
        for i, rows in enumerate((x0, x1)):
            at = pl.ds(pl.multiple_of(jnp.where(near, i, 1 - i) * 192, 192), 192)
            part[at, :] = jnp.dot(rows[...], w[...], preferred_element_type=F32)
        part[384:576, :] = jnp.dot(x2[...], w[...], preferred_element_type=F32)
        part[576:768, :] = jnp.dot(x3[...], w[...], preferred_element_type=F32)
        part[768:832, :] = jnp.dot(xp[...], w[...], preferred_element_type=F32)
        part[832:896, :] = jnp.zeros((64, 384), F32)
        for i in range(6):
            at = slice(i * 128, (i + 1) * 128)
            q_ref[at, :] = head_norm(part[at, :128], qg_ref[...])
            kv_ref[at, :] = head_norm(part[at, 128:256], kg_ref[...])
            kv_ref[768 + i * 128 : 896 + i * 128, :] = jnp.transpose(part[at, 256:]).astype(BF)
        pk_ref[...] = head_norm(part[768:832, 128:256], kg_ref[...])
        pvt_ref[...] = jnp.transpose(part[768:896, 256:])[:, :64].astype(BF)

    shape = jax.ShapeDtypeStruct
    return pl.pallas_call(
        kernel,
        out_shape=(shape((768, 128), BF), shape((1536, 128), BF), shape((64, 128), BF), shape((128, 64), BF)),
        in_specs=[SMEM] + [FULL] * 11,
        out_specs=(FULL,) * 4,
        scratch_shapes=[pltpu.VMEM((3072, 384), BF), pltpu.VMEM((896, 384), F32)],
        compiler_params=params(),
        cost_estimate=cost(6),
        name="project",
    )(flags, query_gain, key_gain, *inputs, prompt_inputs, *weight_pieces)


def attend(queries, pairs, prompt, sums, last):
    tile = 256
    n, m = len(queries), len(pairs)

    def kernel(*refs):
        refs = list(refs)
        q_refs, rest = refs[:n], refs[n:]
        kv_refs = []
        for pair in pairs:
            kv_refs.append((rest[0], rest[len(pair) - 1], 768 * (len(pair) == 1)))
            rest = rest[len(pair) :]
        if prompt:
            pk, pv, pw = rest[:3]
            rest = rest[3:]
        sum_refs = rest[: len(sums)]
        out_refs = rest[len(sums) :]
        for i in range(n):
            for t in range(768 // tile):
                at = slice(t * tile, (t + 1) * tile)
                query = q_refs[i][at, :]
                if sums:
                    numer, denom = sum_refs[i][0:128, at], sum_refs[i][128:136, at]
                else:
                    numer, denom = jnp.zeros((128, tile), F32), jnp.zeros((8, tile), F32)
                for keys, values, start in kv_refs:
                    scores = lax.dot_general(keys[0:768, :], query, NT, preferred_element_type=F32)
                    expon = jnp.exp2(scores * EXP2_SCALE)
                    denom = denom + jnp.sum(expon.reshape(96, 8, tile), axis=0)
                    value = jnp.concatenate([values[start + 128 * j : start + 128 * (j + 1), :] for j in range(6)], axis=1)
                    numer = numer + jnp.dot(value, expon.astype(BF), preferred_element_type=F32)
                if prompt:
                    scores = lax.dot_general(pk[...], query, NT, preferred_element_type=F32)
                    expon = jnp.exp2(scores * EXP2_SCALE) * pw[:, :1]
                    denom = denom + jnp.sum(expon.reshape(8, 8, tile), axis=0)
                    numer = numer + jnp.dot(pv[...], expon.astype(BF), preferred_element_type=F32)
                if last:
                    total = jnp.sum(denom, axis=0, keepdims=True)
                    high = total.astype(BF).astype(F32)
                    out_refs[i][0:128, at] = numer.astype(BF)
                    low = jnp.concatenate([high, total - high, jnp.zeros((14, tile), F32)], axis=0)
                    out_refs[i][128:144, at] = low.astype(BF)
                else:
                    out_refs[i][0:128, at] = numer
                    out_refs[i][128:136, at] = denom

    out = jax.ShapeDtypeStruct((144, 768), BF) if last else jax.ShapeDtypeStruct((136, 768), F32)
    args = [*queries, *[part for pair in pairs for part in pair], *prompt, *sums]
    return pl.pallas_call(
        kernel,
        out_shape=(out,) * n,
        in_specs=[FULL] * len(args),
        out_specs=(FULL,) * n,
        compiler_params=params(),
        cost_estimate=cost(0.7 * n * m),
        name="attend",
    )(*args)


def combine(parts):
    def kernel(a, b, c, d, *out_refs):
        parts = [r[...].astype(F32) for r in (a, b, c, d)]
        total = parts[0] + parts[1] + parts[2] + parts[3]
        denom = total[128:129, :] + total[129:130, :]
        rows = jnp.transpose(total[:128, :] / denom).astype(BF)
        for i, out_ref in enumerate(out_refs):
            out_ref[...] = rows[192 * i : 192 * (i + 1), :]

    return pl.pallas_call(
        kernel,
        out_shape=(jax.ShapeDtypeStruct((192, 128), BF),) * 4,
        in_specs=[FULL] * 4,
        out_specs=(FULL,) * 4,
        compiler_params=params(),
        cost_estimate=cost(0.5),
        name="combine",
    )(*parts)


def project_out(flags, gathered, weight_pieces, gate):
    def kernel(flags_ref, near0, near1, near2, near3, across, far, w0, w1, w2, w3, gate_ref, out_ref, rows, weight):
        z_lo, core, z_hi = flags_ref[0], flags_ref[1], flags_ref[4]
        for block, source in gathered_blocks(flags_ref, (w0, w1, w2, w3), 0):
            weight[block // 4, pl.ds(pl.multiple_of(block % 4 * 192, 192), 192), :] = source
        for i in range(16):
            cross, other, r = i // 8, (i // 4) % 2, i % 4
            low = jnp.where(other == 0, z_lo, 1 - z_lo)
            head_group = low * 2 + jnp.where(cross == 0, core, 1 - core)
            turn = {0: 0, 1: 1 - 2 * low, 2: 2 * low - 1, 3: 2}[r]
            member = (z_hi + 4 + turn) % 4
            if i < 4:
                src, start = (near0, near1, near2, near3)[i], 0
            else:
                src, start = (across, 0) if i < 8 else (far, (i // 4 - 2) * 768)
                start += r * 192

            @pl.when(member < 3)
            def _():
                at = pl.multiple_of(head_group * 384 + member * 128, 128)
                rows[:, pl.ds(at, 128)] = src[start : start + 192, :]

        total = jnp.zeros((192, 768), F32)
        for h in range(4):
            total = total + lax.dot_general(rows[:, h * 384 : (h + 1) * 384], weight[h], NT, preferred_element_type=F32)
        out_ref[...] = (total * gate_ref[...]).astype(BF)

    return pl.pallas_call(
        kernel,
        out_shape=jax.ShapeDtypeStruct((192, 768), BF),
        in_specs=[SMEM] + [FULL] * 11,
        out_specs=FULL,
        scratch_shapes=[pltpu.VMEM((192, 1536), BF), pltpu.VMEM((4, 768, 384), BF)],
        compiler_params=params(),
        cost_estimate=cost(3),
        name="project_out",
    )(flags, *gathered, *weight_pieces, gate)


def head_columns(flags, weight, turned):
    def kernel(flags_ref, weight_ref, turned_ref, *refs):
        out_refs, sems = refs[:4], refs[4]
        copies = []
        for k, out_ref in enumerate(out_refs):
            member = jnp.minimum((flags_ref[4] + k) % 4, 2)
            at = pl.ds(pl.multiple_of(member * 384, 128), 384)
            copies.append(pltpu.make_async_copy(weight_ref.at[:, at], out_ref.at[pl.ds(0, 48), :], sems.at[k]))
            copies.append(pltpu.make_async_copy(turned_ref, out_ref.at[pl.ds(48, 48), :], sems.at[4 + k]))
        for copy in copies:
            copy.start()
        for copy in copies:
            copy.wait()

    return pl.pallas_call(
        kernel,
        out_shape=(jax.ShapeDtypeStruct((96, 384), BF),) * 4,
        in_specs=[SMEM, HBM, ANY],
        out_specs=(FULL,) * 4,
        scratch_shapes=[pltpu.SemaphoreType.DMA((8,))],
        compiler_params=params(),
        cost_estimate=cost(0.3),
        name="head_columns",
    )(flags, weight, turned)


def by_z_hi(flags, blocks):
    def kernel(flags_ref, b0, b1, b3, b2, upper_ref, lower_ref):
        for k, block in enumerate((b0, b1, b2, b3)):
            at = pl.ds(pl.multiple_of((flags_ref[4] + 4 - k) % 4 * 48, 16), 48)
            upper_ref[at, :] = block[0:48, :]
            lower_ref[at, :] = block[48:96, :]

    return pl.pallas_call(
        kernel,
        out_shape=(jax.ShapeDtypeStruct((192, 384), BF),) * 2,
        in_specs=[SMEM] + [FULL] * 4,
        out_specs=(FULL,) * 2,
        compiler_params=params(),
        cost_estimate=cost(0.5),
        name="by_z_hi",
    )(flags, *blocks)


def over(arrays):
    rows, width = arrays[0].shape

    def kernel(*refs):
        for i, ref in enumerate(refs[:-1]):
            refs[-1][i * rows : (i + 1) * rows, :] = ref[...]

    return pl.pallas_call(
        kernel,
        out_shape=jax.ShapeDtypeStruct((len(arrays) * rows, width), arrays[0].dtype),
        in_specs=[FULL] * len(arrays),
        out_specs=FULL,
        compiler_params=params(),
        cost_estimate=cost(0.4),
        name="over",
    )(*arrays)


def after(value, *others):
    return lax.optimization_barrier((value, *others))[0]


def together(*values):
    return lax.optimization_barrier(values)


def body(tokens, prompt, prompt_mask, shift_vec, scale_vec, gate_vec, qkv_weight, query_gain, key_gain, out_weight):
    seq, head = lax.axis_index("seq"), lax.axis_index("head")
    y, x, z_hi, z_lo, core = seq // 16, (seq // 4) % 4, seq % 4, head // 2, head % 2
    flags = jnp.stack([z_lo, core, y, x, z_hi]).astype(jnp.int32)
    shift, gain = shift_vec[None], scale_vec[None]
    prompt_weight = lax.dynamic_slice(prompt_mask, (64 * y,), (64,)).astype(F32)
    prompt_weight = jnp.broadcast_to(prompt_weight[:, None], (64, 128))

    def along(k, core_x):
        return lambda y, x, z, c: (y, x + k, z, c) if c == core_x else (y + k, x, z, c)

    rows = head_columns(flags, qkv_weight, jnp.transpose(out_weight))
    rows = [rows[0]] + [send(rows[k], lambda y, x, z, c: (y, x, z + 2 * k, c)) for k in (1, 3, 2)]
    sibling, a1, *rows = together(to_sibling(tokens), round_z(tokens), *rows)

    column, out_column = by_z_hi(flags, rows)
    line = [send(column, along(k, 0)) for k in (1, 3, 2)]
    a2, b1, column, *line = together(round_z(a1), round_z(sibling), column, *line)

    line = over([column] + line)
    weight1, weight3 = [send(line, along(k, 1)) for k in (1, 3)]
    prompt_inputs = modulate_prompt(after(prompt, line), flags, shift, gain)
    swap = [(d, device_at(d % 4, x, z // 2 * 2 + y // 2, y % 2)) for d in range(256) for y, x, z, c in [place(d)]]
    out_column = lax.ppermute(out_column, AX, swap)
    a3, b2, line, weight1, weight3, prompt_inputs, prompt_weight, out_column = together(
        round_z(a2), round_z(b1), line, weight1, weight3, prompt_inputs, prompt_weight, out_column
    )

    rows1 = modulate_block((tokens, sibling, a1, b1, a2, b2), first_blocks, flags, shift, gain, 4)
    out_line = [send(out_column, along(k, 0)) for k in (1, 3, 2)]
    a4, b3, weight2, rows1, out_column, *out_line = together(
        round_z(a3), round_z(b2), send(line, along(2, 1)), rows1, out_column, *out_line
    )

    other = to_sibling(over([a2, b2, a3, b3, a4]))
    sibling1 = to_sibling(rows1)
    out_line = over([out_column] + out_line)
    out1, out3 = [send(out_line, along(k, 1)) for k in (1, 3)]
    rows3 = modulate_block((a2, b2, a3, b3, other), third_blocks, flags, shift, gain)
    rows4 = modulate_block((a3, b3, a4, other), last_blocks, flags, shift, gain)
    inputs = [rows1, sibling1, rows3, rows4]
    weight_pieces = [line, weight1, weight3, weight2]
    q, kv, pk, pvt = project(flags, inputs, prompt_inputs, weight_pieces, query_gain[None], key_gain[None])

    q, kv, out1, out3, out_line = together(q, kv, out1, out3, out_line)
    kv1, kv3 = [send(kv, lambda y, x, z, c: (y, x + n, z, c)) for n in (1, 3)]
    q1, q3 = [send(q, lambda y, x, z, c: (y + n, x, z, c)) for n in (1, 3)]
    kv1, kv3, q1, q3 = together(kv1, kv3, q1, q3)
    kv2 = send(after(kv, kv1), lambda y, x, z, c: (y, x + 2, z, c))
    q2 = send(after(q, kv1), lambda y, x, z, c: (y + 2, x, z, c))
    prompt_parts = (pk, pvt, prompt_weight)
    sums = attend((q1, q3, q), ((kv,), (kv1,), (kv3,)), prompt_parts, (), False)
    q2, kv2, *sums = together(q2, kv2, *sums)
    (part2,) = attend((q2,), ((kv,), (kv1,), (kv3,), (kv2,)), prompt_parts, (), True)
    part1, part3, part0 = attend((q1, q3, q), ((kv2,),), (), sums, True)
    parts = [part0] + [send(p, lambda y, x, z, c: (y - n, x, z, c)) for n, p in ((2, part2), (1, part1), (3, part3))]
    attended = combine(parts)

    def turn(n):
        step = {1: lambda low: -1 + 2 * low, 2: lambda low: 1 - 2 * low, 3: lambda low: 2}[n]
        return lambda y, x, z, c: (y, x, z + 2 * step(z % 2), c)

    near = [attended[0]] + [send(attended[n], turn(n)) for n in (1, 2, 3)]
    out2 = send(after(out_line, attended[0]), along(2, 1))
    *near, out2 = together(*near, out2)
    blocks = over(near)
    across = send(blocks, lambda y, x, z, c: (y, x, z ^ 1, c))
    gathered = (*near, across, to_sibling(over([blocks, across])))
    return project_out(flags, gathered, [out_line, out1, out3, out2], gate_vec[None])


def solution(mesh):
    placed = (P("seq", "head"), P(), P(), P(), P(), P("head"), P("seq", "head"), P(), P(), P("head", "seq"))
    return jax.shard_map(body, mesh=mesh, in_specs=placed, out_specs=P("seq", "head"), check_vma=False)
```

```python
import math

import jax
import jax.numpy as jnp
from jax import lax
from jax.experimental import pallas as pl
from jax.experimental.pallas import tpu as pltpu
from jax.sharding import PartitionSpec as P

AX = ("seq", "head")
ORDER = (0, 1, 3, 2)
BF = jnp.bfloat16
F32 = jnp.float32
NT = (((1,), (1,)), ((), ()))
EXP2_SCALE = math.log2(math.e) / math.sqrt(128.0)
VMEM = 20 << 20
ANY = pl.BlockSpec(memory_space=pl.ANY)
SMEM = pl.BlockSpec(memory_space=pltpu.SMEM)
FULL = pl.BlockSpec(memory_space=pltpu.VMEM)
HBM = pl.BlockSpec(memory_space=pltpu.HBM)


def place(device):
    seq, head = divmod(device, 4)
    return seq // 16, (seq // 4) % 4, (seq % 4) * 2 + head // 2, head % 2


def device_at(y, x, z, core):
    y, x, z = y % 4, x % 4, z % 8
    return (y * 16 + x * 4 + z // 2) * 4 + (z % 2) * 2 + core


def send(value, target):
    pairs = [(d, device_at(*target(*place(d)))) for d in range(256)]
    return lax.ppermute(value, AX, pairs)


def to_sibling(value):
    return send(value, lambda y, x, z, c: (y, x, z, 1 - c))


def round_z(value):
    return send(value, lambda y, x, z, c: (y, x, z + 1 - 2 * c, c))


def cost(microseconds):
    return pl.CostEstimate(flops=0, bytes_accessed=int(microseconds * 3e6), transcendentals=0)


def params():
    return pltpu.CompilerParams(vmem_limit_bytes=VMEM)


def first_blocks(z_lo, core):
    near = z_lo != core
    chips = [[(0, 0), (1, 0)], [(2, 0), (3, 192)], [(3, 0), (4, 192)]]
    first, second = chips[0:2] if near else chips[1:3]
    if (z_lo == 1) == near:
        first, second = second, first
    return [chip[f ^ core] for chip in (first, second) for f in (0, 1)]


def third_blocks(z_lo, core):
    mine = [[(0, 0), (1, 192)], [(1, 0), (2, 192)]]
    other = [[(3, 0), (3, 384)], [(3, 192), (3, 768)]]
    near = z_lo != core
    first, second = [[chip[f ^ core if near else f ^ core ^ 1] for f in (0, 1)] for chip in (mine if near else other)]
    return first + second if z_lo == 0 else second + first


def last_blocks(z_lo, core):
    far = z_lo == core
    third = [[(0, 0), (1, 192)][f ^ core] if far else [(2, 192), (2, 768)][f ^ core ^ 1] for f in (0, 1)]
    fourth = [(1, 0) if f == core else (2, 576) for f in (0, 1)]
    return fourth + third if z_lo == 0 else third + fourth


def modulate_rows(rows, step, load, shift_ref, gain_ref, out_ref):
    @pl.loop(0, rows // step)
    def _(i):
        at = pl.ds(pl.multiple_of(i * step, step), step)
        total = jnp.zeros((step, 128), F32)
        for b in range(24):
            total = total + load(at, b)
        center = jnp.sum(total, axis=1, keepdims=True) * (1.0 / 3072)
        total = jnp.zeros((step, 128), F32)
        for b in range(24):
            value = load(at, b) - center
            total = total + value * value
        scale = lax.rsqrt(jnp.sum(total, axis=1, keepdims=True) * (1.0 / 3072) + 1e-06)
        for b in range(24):
            cols = slice(b * 128, (b + 1) * 128)
            out_ref[at, cols] = ((load(at, b) - center) * scale * (1.0 + gain_ref[:, cols]) + shift_ref[:, cols]).astype(BF)


def modulate_block(sources, choose, flags, shift, gain, far_sources=0):
    count = len(sources)

    def kernel(flags_ref, shift_ref, gain_ref, *refs):
        out_ref, buf, sems = refs[count:]
        for z_lo in (0, 1):
            for core in (0, 1):

                @pl.when((flags_ref[0] == z_lo) & (flags_ref[1] == core))
                def _():
                    copies = []
                    for b, source in enumerate(choose(z_lo, core)):
                        source, start = source
                        cols = slice(b * 768, (b + 1) * 768)
                        if source < far_sources:
                            copies.append(pltpu.make_async_copy(refs[source], buf.at[:, cols], sems.at[b]))
                            copies[-1].start()
                        else:
                            buf[:, cols] = refs[source][start : start + 192, :]
                    for copy in copies:
                        copy.wait()

        load = lambda at, b: buf[at, b * 128 : (b + 1) * 128].astype(F32)
        modulate_rows(192, 64, load, shift_ref, gain_ref, out_ref)

    return pl.pallas_call(
        kernel,
        out_shape=jax.ShapeDtypeStruct((192, 3072), BF),
        in_specs=[SMEM, FULL, FULL] + [HBM] * far_sources + [FULL] * (count - far_sources),
        out_specs=FULL,
        scratch_shapes=[pltpu.VMEM((192, 3072), BF), pltpu.SemaphoreType.DMA((4,))],
        compiler_params=params(),
        cost_estimate=cost(6),
        name="modulate",
    )(flags, shift, gain, *sources)


def modulate_prompt(prompt, flags, shift, gain):
    def kernel(flags_ref, shift_ref, gain_ref, prompt_ref, out_ref, buf, sem):
        at = pl.multiple_of(flags_ref[2] * 64, 64)
        copy = pltpu.make_async_copy(prompt_ref.at[pl.ds(at, 64), :], buf, sem)
        copy.start()
        copy.wait()
        load = lambda rows, b: buf[rows, b * 128 : (b + 1) * 128].astype(F32)
        modulate_rows(64, 64, load, shift_ref, gain_ref, out_ref)

    return pl.pallas_call(
        kernel,
        out_shape=jax.ShapeDtypeStruct((64, 3072), BF),
        in_specs=[SMEM, FULL, FULL, HBM],
        out_specs=FULL,
        scratch_shapes=[pltpu.VMEM((64, 3072), BF), pltpu.SemaphoreType.DMA],
        compiler_params=params(),
        cost_estimate=cost(6),
        name="modulate_prompt",
    )(flags, shift, gain, prompt)


def head_norm(values, gain):
    power = jnp.mean(values * values, axis=1, keepdims=True)
    return (values * lax.rsqrt(power + 1e-06) * gain).astype(BF)


def gathered_blocks(flags_ref, pieces, x_inside):
    core, y, x = flags_ref[1], flags_ref[2], flags_ref[3]
    for outer, piece in enumerate(pieces):
        for inner in range(4):
            dx = jnp.where(core == x_inside, ORDER[inner], ORDER[outer])
            dy = jnp.where(core == x_inside, ORDER[outer], ORDER[inner])
            block = ((y + 4 - dy) % 4) * 4 + (x + 4 - dx) % 4
            yield block, piece[inner * 192 : (inner + 1) * 192, :]


def project(flags, inputs, prompt_inputs, weight_pieces, query_gain, key_gain):
    def kernel(flags_ref, qg_ref, kg_ref, x0, x1, x2, x3, xp, w0, w1, w2, w3, q_ref, kv_ref, pk_ref, pvt_ref, w, part):
        for block, source in gathered_blocks(flags_ref, (w0, w1, w2, w3), 0):
            w[pl.ds(pl.multiple_of(block * 192, 192), 192), :] = source
        near = flags_ref[0] != flags_ref[1]
        for i, rows in enumerate((x0, x1)):
            at = pl.ds(pl.multiple_of(jnp.where(near, i, 1 - i) * 192, 192), 192)
            part[at, :] = jnp.dot(rows[...], w[...], preferred_element_type=F32)
        part[384:576, :] = jnp.dot(x2[...], w[...], preferred_element_type=F32)
        part[576:768, :] = jnp.dot(x3[...], w[...], preferred_element_type=F32)
        part[768:832, :] = jnp.dot(xp[...], w[...], preferred_element_type=F32)
        part[832:896, :] = jnp.zeros((64, 384), F32)
        for i in range(6):
            at = slice(i * 128, (i + 1) * 128)
            q_ref[at, :] = head_norm(part[at, :128], qg_ref[...])
            kv_ref[at, :] = head_norm(part[at, 128:256], kg_ref[...])
            kv_ref[768 + i * 128 : 896 + i * 128, :] = jnp.transpose(part[at, 256:]).astype(BF)
        pk_ref[...] = head_norm(part[768:832, 128:256], kg_ref[...])
        pvt_ref[...] = jnp.transpose(part[768:896, 256:])[:, :64].astype(BF)

    shape = jax.ShapeDtypeStruct
    return pl.pallas_call(
        kernel,
        out_shape=(shape((768, 128), BF), shape((1536, 128), BF), shape((64, 128), BF), shape((128, 64), BF)),
        in_specs=[SMEM] + [FULL] * 11,
        out_specs=(FULL,) * 4,
        scratch_shapes=[pltpu.VMEM((3072, 384), BF), pltpu.VMEM((896, 384), F32)],
        compiler_params=params(),
        cost_estimate=cost(6),
        name="project",
    )(flags, query_gain, key_gain, *inputs, prompt_inputs, *weight_pieces)


def attend(queries, pairs, prompt, sums, last):
    tile = 256
    n, m = len(queries), len(pairs)

    def kernel(*refs):
        refs = list(refs)
        q_refs, rest = refs[:n], refs[n:]
        kv_refs = []
        for pair in pairs:
            kv_refs.append((rest[0], rest[len(pair) - 1], 768 * (len(pair) == 1)))
            rest = rest[len(pair) :]
        if prompt:
            pk, pv, pw = rest[:3]
            rest = rest[3:]
        sum_refs = rest[: len(sums)]
        out_refs = rest[len(sums) :]
        for i in range(n):
            for t in range(768 // tile):
                at = slice(t * tile, (t + 1) * tile)
                query = q_refs[i][at, :]
                if sums:
                    numer, denom = sum_refs[i][0:128, at], sum_refs[i][128:136, at]
                else:
                    numer, denom = jnp.zeros((128, tile), F32), jnp.zeros((8, tile), F32)
                for keys, values, start in kv_refs:
                    scores = lax.dot_general(keys[0:768, :], query, NT, preferred_element_type=F32)
                    expon = jnp.exp2(scores * EXP2_SCALE)
                    denom = denom + jnp.sum(expon.reshape(96, 8, tile), axis=0)
                    value = jnp.concatenate([values[start + 128 * j : start + 128 * (j + 1), :] for j in range(6)], axis=1)
                    numer = numer + jnp.dot(value, expon.astype(BF), preferred_element_type=F32)
                if prompt:
                    scores = lax.dot_general(pk[...], query, NT, preferred_element_type=F32)
                    expon = jnp.exp2(scores * EXP2_SCALE) * pw[:, :1]
                    denom = denom + jnp.sum(expon.reshape(8, 8, tile), axis=0)
                    numer = numer + jnp.dot(pv[...], expon.astype(BF), preferred_element_type=F32)
                if last:
                    total = jnp.sum(denom, axis=0, keepdims=True)
                    high = total.astype(BF).astype(F32)
                    out_refs[i][0:128, at] = numer.astype(BF)
                    low = jnp.concatenate([high, total - high, jnp.zeros((14, tile), F32)], axis=0)
                    out_refs[i][128:144, at] = low.astype(BF)
                else:
                    out_refs[i][0:128, at] = numer
                    out_refs[i][128:136, at] = denom

    out = jax.ShapeDtypeStruct((144, 768), BF) if last else jax.ShapeDtypeStruct((136, 768), F32)
    args = [*queries, *[part for pair in pairs for part in pair], *prompt, *sums]
    return pl.pallas_call(
        kernel,
        out_shape=(out,) * n,
        in_specs=[FULL] * len(args),
        out_specs=(FULL,) * n,
        compiler_params=params(),
        cost_estimate=cost(0.7 * n * m),
        name="attend",
    )(*args)


def combine(parts):
    def kernel(a, b, c, d, out_ref):
        parts = [r[...].astype(F32) for r in (a, b, c, d)]
        total = parts[0] + parts[1] + parts[2] + parts[3]
        denom = total[128:129, :] + total[129:130, :]
        out_ref[...] = jnp.transpose(total[:128, :] / denom).astype(BF)

    return pl.pallas_call(
        kernel,
        out_shape=jax.ShapeDtypeStruct((768, 128), BF),
        in_specs=[FULL] * 4,
        out_specs=FULL,
        compiler_params=params(),
        cost_estimate=cost(0.5),
        name="combine",
    )(*parts)


def project_out(flags, near, far, weight_pieces, gate):
    def kernel(flags_ref, near0, near1, near2, near3, far_ref, w0, w1, w2, w3, gate_ref, out_ref, rows, weight):
        z_lo, core, z_hi = flags_ref[0], flags_ref[1], flags_ref[4]
        for block, source in gathered_blocks(flags_ref, (w0, w1, w2, w3), 1):
            weight[block // 4, pl.ds(pl.multiple_of(block % 4 * 192, 192), 192), :] = source

        def put(low, r, ref, start):
            member = (z_hi + 4 + {0: 0, 1: 1 - 2 * low, 2: 2 * low - 1, 3: 2}[r]) % 4

            @pl.when(member < 3)
            def _():
                for half in (0, 1):
                    head_group = low * 2 + (z_lo + half) % 2
                    at = pl.multiple_of(head_group * 384 + member * 128, 128)
                    rows[:, pl.ds(at, 128)] = ref[start + half * 192 : start + half * 192 + 192, :]

        for r, ref in enumerate((near0, near1, near2, near3)):
            put(core, r, ref, 0)
            put(1 - core, r, far_ref, r * 384)
        total = jnp.zeros((192, 768), F32)
        for h in range(4):
            total = total + lax.dot_general(rows[:, h * 384 : (h + 1) * 384], weight[h], NT, preferred_element_type=F32)
        out_ref[...] = (total * gate_ref[...]).astype(BF)

    return pl.pallas_call(
        kernel,
        out_shape=jax.ShapeDtypeStruct((192, 768), BF),
        in_specs=[SMEM] + [FULL] * 10,
        out_specs=FULL,
        scratch_shapes=[pltpu.VMEM((192, 1536), BF), pltpu.VMEM((4, 768, 384), BF)],
        compiler_params=params(),
        cost_estimate=cost(3),
        name="project_out",
    )(flags, *near, far, *weight_pieces, gate)


def first_piece(own, received, flags):
    def kernel(flags_ref, own_ref, received_ref, out_ref):
        @pl.when(flags_ref[0] == flags_ref[1])
        def _():
            out_ref[...] = own_ref[...]

        @pl.when(flags_ref[0] != flags_ref[1])
        def _():
            out_ref[...] = received_ref[...]

    return pl.pallas_call(
        kernel,
        out_shape=jax.ShapeDtypeStruct(own.shape, own.dtype),
        in_specs=[SMEM, FULL, FULL],
        out_specs=FULL,
        compiler_params=params(),
        cost_estimate=cost(0.3),
        name="first_piece",
    )(flags, own, received)


def head_columns(flags, weight, turned):
    def kernel(flags_ref, weight_ref, turned_ref, *refs):
        out_refs, sems = refs[:4], refs[4]
        copies = []
        for k, out_ref in enumerate(out_refs):
            member = jnp.minimum((flags_ref[4] + k) % 4, 2)
            at = pl.ds(pl.multiple_of(member * 384, 128), 384)
            copies.append(pltpu.make_async_copy(weight_ref.at[:, at], out_ref.at[pl.ds(0, 48), :], sems.at[k]))
            copies.append(pltpu.make_async_copy(turned_ref, out_ref.at[pl.ds(48, 48), :], sems.at[4 + k]))
        for copy in copies:
            copy.start()
        for copy in copies:
            copy.wait()

    return pl.pallas_call(
        kernel,
        out_shape=(jax.ShapeDtypeStruct((96, 384), BF),) * 4,
        in_specs=[SMEM, HBM, ANY],
        out_specs=(FULL,) * 4,
        scratch_shapes=[pltpu.SemaphoreType.DMA((8,))],
        compiler_params=params(),
        cost_estimate=cost(0.3),
        name="head_columns",
    )(flags, weight, turned)


def by_z_hi(flags, blocks):
    def kernel(flags_ref, b0, b1, b3, b2, upper_ref, lower_ref):
        for k, block in enumerate((b0, b1, b2, b3)):
            at = pl.ds(pl.multiple_of((flags_ref[4] + 4 - k) % 4 * 48, 16), 48)
            upper_ref[at, :] = block[0:48, :]
            lower_ref[at, :] = block[48:96, :]

    return pl.pallas_call(
        kernel,
        out_shape=(jax.ShapeDtypeStruct((192, 384), BF),) * 2,
        in_specs=[SMEM] + [FULL] * 4,
        out_specs=(FULL,) * 2,
        compiler_params=params(),
        cost_estimate=cost(0.5),
        name="by_z_hi",
    )(flags, *blocks)


def lower(arrays):
    def kernel(*refs):
        for i, ref in enumerate(refs[:-1]):
            refs[-1][i * 192 : (i + 1) * 192, :] = ref[768:960, :]

    return pl.pallas_call(
        kernel,
        out_shape=jax.ShapeDtypeStruct((768, 384), BF),
        in_specs=[FULL] * 4,
        out_specs=FULL,
        compiler_params=params(),
        cost_estimate=cost(0.4),
        name="lower",
    )(*arrays)


def pieces(mine, other):
    def kernel(mine_ref, other_ref, *out_refs):
        for i, out_ref in enumerate(out_refs):
            out_ref[0:192, :] = mine_ref[i * 192 : (i + 1) * 192, :]
            out_ref[192:384, :] = other_ref[i * 192 : (i + 1) * 192, :]

    return pl.pallas_call(
        kernel,
        out_shape=(jax.ShapeDtypeStruct((384, 128), BF),) * 4,
        in_specs=[FULL] * 2,
        out_specs=(FULL,) * 4,
        compiler_params=params(),
        cost_estimate=cost(0.3),
        name="pieces",
    )(mine, other)


def rows_of(parts):
    arrays, counts = zip(*parts)

    def kernel(*refs):
        start = 0
        for count, ref in zip(counts, refs):
            refs[-1][start : start + count, :] = ref[0:count, :]
            start += count

    return pl.pallas_call(
        kernel,
        out_shape=jax.ShapeDtypeStruct((sum(counts), arrays[0].shape[1]), arrays[0].dtype),
        in_specs=[FULL] * len(arrays),
        out_specs=FULL,
        compiler_params=params(),
        cost_estimate=cost(0.4),
        name="rows_of",
    )(*arrays)


def over(arrays):
    return rows_of([(array, array.shape[0]) for array in arrays])


def after(value, *others):
    return lax.optimization_barrier((value, *others))[0]


def together(*values):
    return lax.optimization_barrier(values)


def body(tokens, prompt, prompt_mask, shift_vec, scale_vec, gate_vec, qkv_weight, query_gain, key_gain, out_weight):
    seq, head = lax.axis_index("seq"), lax.axis_index("head")
    y, x, z_hi, z_lo, core = seq // 16, (seq // 4) % 4, seq % 4, head // 2, head % 2
    flags = jnp.stack([z_lo, core, y, x, z_hi]).astype(jnp.int32)
    shift, gain = shift_vec[None], scale_vec[None]
    prompt_weight = lax.dynamic_slice(prompt_mask, (64 * y,), (64,)).astype(F32)
    prompt_weight = jnp.broadcast_to(prompt_weight[:, None], (64, 128))

    def along(k, core_x):
        return lambda y, x, z, c: (y, x + k, z, c) if c == core_x else (y + k, x, z, c)

    rows = head_columns(flags, qkv_weight, jnp.transpose(out_weight))
    rows = [rows[0]] + [send(rows[k], lambda y, x, z, c: (y, x, z + 2 * k, c)) for k in (1, 3, 2)]
    sibling, a1, *rows = together(to_sibling(tokens), round_z(tokens), *rows)

    column, out_column = by_z_hi(flags, rows)
    line = [send(column, along(k, 0)) for k in (1, 3, 2)]
    swap = [(d, device_at(d % 4, x, z // 2 * 2 + y // 2, y % 2)) for d in range(256) for y, x, z, c in [place(d)]]
    out_column = lax.ppermute(out_column, AX, swap)
    ring2, column, out_column, *line = together(round_z(over([a1, sibling])), column, out_column, *line)

    line = over([column] + line + [out_column])
    prompt_inputs = modulate_prompt(after(prompt, line), flags, shift, gain)
    weight1, weight3 = [send(line, along(k, 1)) for k in (1, 3)]
    ring3, line, weight1, weight3, prompt_inputs, prompt_weight = together(
        round_z(ring2), line, weight1, weight3, prompt_inputs, prompt_weight
    )

    rows1 = modulate_block((tokens, sibling, a1, ring2, ring3), first_blocks, flags, shift, gain, 3)
    ring4, weight2, rows1 = together(round_z(ring3), send(line, along(2, 1)), rows1)

    other = to_sibling(rows_of([(ring2, 192), (ring3, 384), (ring4, 384)]))
    sibling1 = to_sibling(rows1)
    weight_pieces = [line, weight1, weight3, weight2]
    out_line = lower(weight_pieces)
    out1, out3 = [send(out_line, along(k, 0)) for k in (1, 3)]
    rows3 = modulate_block((ring2, ring3, ring4, other), third_blocks, flags, shift, gain)
    rows4 = modulate_block((ring3, ring4, other), last_blocks, flags, shift, gain)
    inputs = [rows1, sibling1, rows3, rows4]
    q, kv, pk, pvt = project(flags, inputs, prompt_inputs, weight_pieces, query_gain[None], key_gain[None])

    q, kv, out1, out3, out_line = together(q, kv, out1, out3, out_line)
    kv1, kv3 = [send(kv, lambda y, x, z, c: (y, x + n, z, c)) for n in (1, 3)]
    q1, q3 = [send(q, lambda y, x, z, c: (y + n, x, z, c)) for n in (1, 3)]
    kv1, kv3, q1, q3 = together(kv1, kv3, q1, q3)
    kv2 = send(after(kv, kv1), lambda y, x, z, c: (y, x + 2, z, c))
    q2 = send(after(q, kv1), lambda y, x, z, c: (y + 2, x, z, c))
    prompt_parts = (pk, pvt, prompt_weight)
    sums = attend((q1, q3, q), ((kv,), (kv1,), (kv3,)), prompt_parts, (), False)
    q2, kv2, *sums = together(q2, kv2, *sums)
    (part2,) = attend((q2,), ((kv,), (kv1,), (kv3,), (kv2,)), prompt_parts, (), True)
    part1, part3, part0 = attend((q1, q3, q), ((kv2,),), (), sums, True)
    parts = [part0] + [send(p, lambda y, x, z, c: (y - n, x, z, c)) for n, p in ((2, part2), (1, part1), (3, part3))]
    attended = combine(parts)

    def turn(n):
        step = {0: lambda low: 0, 1: lambda low: -1 + 2 * low, 2: lambda low: 1 - 2 * low, 3: lambda low: 2}[n]
        ends = []
        for d in range(256):
            y, x, z, c = place(d)
            ends.append((d, device_at(y, x, (z // 2 + step(z % 2)) * 2 + c, z % 2)))
        return [(s, t) for s, t in ends if s != t]

    parts = pieces(attended, to_sibling(attended))
    near = [lax.ppermute(parts[n], AX, turn(n)) for n in (0, 1, 2, 3)]
    out2 = send(after(out_line, attended), along(2, 0))
    *near, out2 = together(*near, out2)
    near[0] = first_piece(parts[0], near[0], flags)
    far = to_sibling(over(near))
    return project_out(flags, near, far, [out_line, out1, out3, out2], gate_vec[None])


def solution(mesh):
    placed = (P("seq", "head"), P(), P(), P(), P(), P("head"), P("seq", "head"), P(), P(), P("head", "seq"))
    return jax.shard_map(body, mesh=mesh, in_specs=placed, out_specs=P("seq", "head"), check_vma=False)
```

```python
import math

import jax
import jax.numpy as jnp
from jax import lax
from jax.experimental import pallas as pl
from jax.experimental.pallas import tpu as pltpu
from jax.sharding import PartitionSpec as P

AX = ("seq", "head")
ORDER = (0, 1, 3, 2)
BF = jnp.bfloat16
F32 = jnp.float32
NT = (((1,), (1,)), ((), ()))
EXP2_SCALE = math.log2(math.e) / math.sqrt(128.0)
VMEM = 20 << 20
ANY = pl.BlockSpec(memory_space=pl.ANY)
SMEM = pl.BlockSpec(memory_space=pltpu.SMEM)
FULL = pl.BlockSpec(memory_space=pltpu.VMEM)
HBM = pl.BlockSpec(memory_space=pltpu.HBM)


def place(device):
    seq, head = divmod(device, 4)
    return seq // 16, (seq // 4) % 4, (seq % 4) * 2 + head // 2, head % 2


def device_at(y, x, z, core):
    y, x, z = y % 4, x % 4, z % 8
    return (y * 16 + x * 4 + z // 2) * 4 + (z % 2) * 2 + core


def send(value, target):
    pairs = [(d, device_at(*target(*place(d)))) for d in range(256)]
    return lax.ppermute(value, AX, pairs)


def to_sibling(value):
    return send(value, lambda y, x, z, c: (y, x, z, 1 - c))


def round_z(value):
    return send(value, lambda y, x, z, c: (y, x, z + 1 - 2 * c, c))


def cost(microseconds):
    return pl.CostEstimate(flops=0, bytes_accessed=int(microseconds * 3e6), transcendentals=0)


def params():
    return pltpu.CompilerParams(vmem_limit_bytes=VMEM)


def first_blocks(z_lo, core):
    near = z_lo != core
    chips = [[(0, 0), (1, 0)], [(2, 0), (3, 192)], [(3, 0), (4, 192)]]
    first, second = chips[0:2] if near else chips[1:3]
    if (z_lo == 1) == near:
        first, second = second, first
    return [chip[f ^ core] for chip in (first, second) for f in (0, 1)]


def third_blocks(z_lo, core):
    mine = [[(0, 0), (1, 192)], [(1, 0), (2, 192)]]
    other = [[(3, 0), (3, 384)], [(3, 192), (3, 768)]]
    near = z_lo != core
    first, second = [[chip[f ^ core if near else f ^ core ^ 1] for f in (0, 1)] for chip in (mine if near else other)]
    return first + second if z_lo == 0 else second + first


def last_blocks(z_lo, core):
    far = z_lo == core
    third = [[(0, 0), (1, 192)][f ^ core] if far else [(2, 192), (2, 768)][f ^ core ^ 1] for f in (0, 1)]
    fourth = [(1, 0) if f == core else (2, 576) for f in (0, 1)]
    return fourth + third if z_lo == 0 else third + fourth


def modulate_rows(rows, step, load, shift_ref, gain_ref, out_ref):
    @pl.loop(0, rows // step)
    def _(i):
        at = pl.ds(pl.multiple_of(i * step, step), step)
        total = jnp.zeros((step, 128), F32)
        for b in range(24):
            total = total + load(at, b)
        center = jnp.sum(total, axis=1, keepdims=True) * (1.0 / 3072)
        total = jnp.zeros((step, 128), F32)
        for b in range(24):
            value = load(at, b) - center
            total = total + value * value
        scale = lax.rsqrt(jnp.sum(total, axis=1, keepdims=True) * (1.0 / 3072) + 1e-06)
        for b in range(24):
            cols = slice(b * 128, (b + 1) * 128)
            out_ref[at, cols] = ((load(at, b) - center) * scale * (1.0 + gain_ref[:, cols]) + shift_ref[:, cols]).astype(BF)


def modulate_block(sources, choose, flags, shift, gain, far_sources=0):
    count = len(sources)

    def kernel(flags_ref, shift_ref, gain_ref, *refs):
        out_ref, buf, sems = refs[count:]
        for z_lo in (0, 1):
            for core in (0, 1):

                @pl.when((flags_ref[0] == z_lo) & (flags_ref[1] == core))
                def _():
                    copies = []
                    for b, source in enumerate(choose(z_lo, core)):
                        source, start = source
                        cols = slice(b * 768, (b + 1) * 768)
                        if source < far_sources:
                            copies.append(pltpu.make_async_copy(refs[source], buf.at[:, cols], sems.at[b]))
                            copies[-1].start()
                        else:
                            buf[:, cols] = refs[source][start : start + 192, :]
                    for copy in copies:
                        copy.wait()

        load = lambda at, b: buf[at, b * 128 : (b + 1) * 128].astype(F32)
        modulate_rows(192, 96, load, shift_ref, gain_ref, out_ref)

    return pl.pallas_call(
        kernel,
        out_shape=jax.ShapeDtypeStruct((192, 3072), BF),
        in_specs=[SMEM, FULL, FULL] + [HBM] * far_sources + [FULL] * (count - far_sources),
        out_specs=FULL,
        scratch_shapes=[pltpu.VMEM((192, 3072), BF), pltpu.SemaphoreType.DMA((4,))],
        compiler_params=params(),
        cost_estimate=cost(6),
        name="modulate",
    )(flags, shift, gain, *sources)


def modulate_prompt(prompt, flags, shift, gain):
    def kernel(flags_ref, shift_ref, gain_ref, prompt_ref, out_ref, buf, sem):
        at = pl.multiple_of(flags_ref[2] * 64, 64)
        copy = pltpu.make_async_copy(prompt_ref.at[pl.ds(at, 64), :], buf, sem)
        copy.start()
        copy.wait()
        load = lambda rows, b: buf[rows, b * 128 : (b + 1) * 128].astype(F32)
        modulate_rows(64, 64, load, shift_ref, gain_ref, out_ref)

    return pl.pallas_call(
        kernel,
        out_shape=jax.ShapeDtypeStruct((64, 3072), BF),
        in_specs=[SMEM, FULL, FULL, HBM],
        out_specs=FULL,
        scratch_shapes=[pltpu.VMEM((64, 3072), BF), pltpu.SemaphoreType.DMA],
        compiler_params=params(),
        cost_estimate=cost(6),
        name="modulate_prompt",
    )(flags, shift, gain, prompt)


def head_norm(values, gain):
    power = jnp.mean(values * values, axis=1, keepdims=True)
    return (values * lax.rsqrt(power + 1e-06) * gain).astype(BF)


def gathered_blocks(flags_ref, pieces, x_inside):
    core, y, x = flags_ref[1], flags_ref[2], flags_ref[3]
    for outer, piece in enumerate(pieces):
        for inner in range(4):
            dx = jnp.where(core == x_inside, ORDER[inner], ORDER[outer])
            dy = jnp.where(core == x_inside, ORDER[outer], ORDER[inner])
            block = ((y + 4 - dy) % 4) * 4 + (x + 4 - dx) % 4
            yield block, piece[inner * 192 : (inner + 1) * 192, :]


def project(flags, inputs, prompt_inputs, weight_pieces, query_gain, key_gain):
    def kernel(flags_ref, qg_ref, kg_ref, x0, x1, x2, x3, xp, w0, w1, w2, w3, q_ref, kv_ref, pk_ref, pvt_ref, w, part):
        for block, source in gathered_blocks(flags_ref, (w0, w1, w2, w3), 0):
            w[pl.ds(pl.multiple_of(block * 192, 192), 192), :] = source
        near = flags_ref[0] != flags_ref[1]
        for i, rows in enumerate((x0, x1)):
            at = pl.ds(pl.multiple_of(jnp.where(near, i, 1 - i) * 192, 192), 192)
            part[at, :] = jnp.dot(rows[...], w[...], preferred_element_type=F32)
        part[384:576, :] = jnp.dot(x2[...], w[...], preferred_element_type=F32)
        part[576:768, :] = jnp.dot(x3[...], w[...], preferred_element_type=F32)
        part[768:832, :] = jnp.dot(xp[...], w[...], preferred_element_type=F32)
        part[832:896, :] = jnp.zeros((64, 384), F32)
        for i in range(6):
            at = slice(i * 128, (i + 1) * 128)
            q_ref[at, :] = head_norm(part[at, :128], qg_ref[...])
            kv_ref[at, :] = head_norm(part[at, 128:256], kg_ref[...])
            kv_ref[768 + i * 128 : 896 + i * 128, :] = jnp.transpose(part[at, 256:]).astype(BF)
        pk_ref[...] = head_norm(part[768:832, 128:256], kg_ref[...])
        pvt_ref[...] = jnp.transpose(part[768:896, 256:])[:, :64].astype(BF)

    shape = jax.ShapeDtypeStruct
    return pl.pallas_call(
        kernel,
        out_shape=(shape((768, 128), BF), shape((1536, 128), BF), shape((64, 128), BF), shape((128, 64), BF)),
        in_specs=[SMEM] + [FULL] * 11,
        out_specs=(FULL,) * 4,
        scratch_shapes=[pltpu.VMEM((3072, 384), BF), pltpu.VMEM((896, 384), F32)],
        compiler_params=params(),
        cost_estimate=cost(6),
        name="project",
    )(flags, query_gain, key_gain, *inputs, prompt_inputs, *weight_pieces)


def attend(queries, pairs, prompt, sums, last):
    tile = 768
    n, m = len(queries), len(pairs)

    def kernel(*refs):
        refs = list(refs)
        q_refs, rest = refs[:n], refs[n:]
        kv_refs = []
        for pair in pairs:
            kv_refs.append((rest[0], rest[len(pair) - 1], 768 * (len(pair) == 1)))
            rest = rest[len(pair) :]
        if prompt:
            pk, pv, pw = rest[:3]
            rest = rest[3:]
        sum_refs = rest[: len(sums)]
        out_refs = rest[len(sums) :]
        for i in range(n):
            for t in range(768 // tile):
                at = slice(t * tile, (t + 1) * tile)
                query = q_refs[i][at, :]
                if sums:
                    numer, denom = sum_refs[i][0:128, at], sum_refs[i][128:136, at]
                else:
                    numer, denom = jnp.zeros((128, tile), F32), jnp.zeros((8, tile), F32)
                for keys, values, start in kv_refs:
                    scores = lax.dot_general(keys[0:768, :], query, NT, preferred_element_type=F32)
                    expon = jnp.exp2(scores * EXP2_SCALE)
                    denom = denom + jnp.sum(expon.reshape(96, 8, tile), axis=0)
                    value = jnp.concatenate([values[start + 128 * j : start + 128 * (j + 1), :] for j in range(6)], axis=1)
                    numer = numer + jnp.dot(value, expon.astype(BF), preferred_element_type=F32)
                if prompt:
                    scores = lax.dot_general(pk[...], query, NT, preferred_element_type=F32)
                    expon = jnp.exp2(scores * EXP2_SCALE) * pw[:, :1]
                    denom = denom + jnp.sum(expon.reshape(8, 8, tile), axis=0)
                    numer = numer + jnp.dot(pv[...], expon.astype(BF), preferred_element_type=F32)
                if last:
                    total = jnp.sum(denom, axis=0, keepdims=True)
                    high = total.astype(BF).astype(F32)
                    out_refs[i][0:128, at] = numer.astype(BF)
                    low = jnp.concatenate([high, total - high, jnp.zeros((14, tile), F32)], axis=0)
                    out_refs[i][128:144, at] = low.astype(BF)
                else:
                    out_refs[i][0:128, at] = numer
                    out_refs[i][128:136, at] = denom

    out = jax.ShapeDtypeStruct((144, 768), BF) if last else jax.ShapeDtypeStruct((136, 768), F32)
    args = [*queries, *[part for pair in pairs for part in pair], *prompt, *sums]
    return pl.pallas_call(
        kernel,
        out_shape=(out,) * n,
        in_specs=[FULL] * len(args),
        out_specs=(FULL,) * n,
        compiler_params=params(),
        cost_estimate=cost(0.7 * n * m),
        name="attend",
    )(*args)


def combine(parts):
    def kernel(a, b, c, d, out_ref):
        parts = [r[...].astype(F32) for r in (a, b, c, d)]
        total = parts[0] + parts[1] + parts[2] + parts[3]
        denom = total[128:129, :] + total[129:130, :]
        out_ref[...] = jnp.transpose(total[:128, :] / denom).astype(BF)

    return pl.pallas_call(
        kernel,
        out_shape=jax.ShapeDtypeStruct((768, 128), BF),
        in_specs=[FULL] * 4,
        out_specs=FULL,
        compiler_params=params(),
        cost_estimate=cost(0.5),
        name="combine",
    )(*parts)


def project_out(flags, near, far, weight_pieces, gate):
    def kernel(flags_ref, near_ref, far_ref, w0, w1, w2, w3, gate_ref, out_ref, rows, weight):
        z_lo, core, z_hi = flags_ref[0], flags_ref[1], flags_ref[4]
        for block, source in gathered_blocks(flags_ref, (w0, w1, w2, w3), 1):
            weight[block // 4, pl.ds(pl.multiple_of(block % 4 * 192, 192), 192), :] = source

        def put(low, r, ref, start):
            member = (z_hi + 4 + {0: 0, 1: 1 - 2 * low, 2: 2 * low - 1, 3: 2}[r]) % 4

            @pl.when(member < 3)
            def _():
                for half in (0, 1):
                    head_group = low * 2 + (z_lo + half) % 2
                    at = pl.multiple_of(head_group * 384 + member * 128, 128)
                    rows[:, pl.ds(at, 128)] = ref[start + half * 192 : start + half * 192 + 192, :]

        for r in (0, 1, 2, 3):
            put(core, r, near_ref, r * 384)
            put(1 - core, r, far_ref, r * 384)
        total = jnp.zeros((192, 768), F32)
        for h in range(4):
            total = total + lax.dot_general(rows[:, h * 384 : (h + 1) * 384], weight[h], NT, preferred_element_type=F32)
        out_ref[...] = (total * gate_ref[...]).astype(BF)

    return pl.pallas_call(
        kernel,
        out_shape=jax.ShapeDtypeStruct((192, 768), BF),
        in_specs=[SMEM] + [FULL] * 7,
        out_specs=FULL,
        scratch_shapes=[pltpu.VMEM((192, 1536), BF), pltpu.VMEM((4, 768, 384), BF)],
        compiler_params=params(),
        cost_estimate=cost(3),
        name="project_out",
    )(flags, near, far, *weight_pieces, gate)


def all_pieces(flags, own, received):
    def kernel(flags_ref, own_ref, *refs):
        out_ref = refs[4]

        @pl.when(flags_ref[0] == flags_ref[1])
        def _():
            out_ref[0:384, :] = own_ref[...]

        @pl.when(flags_ref[0] != flags_ref[1])
        def _():
            out_ref[0:384, :] = refs[0][...]

        for r in (1, 2, 3):
            out_ref[r * 384 : (r + 1) * 384, :] = refs[r][...]

    return pl.pallas_call(
        kernel,
        out_shape=jax.ShapeDtypeStruct((1536, 128), BF),
        in_specs=[SMEM] + [FULL] * 5,
        out_specs=FULL,
        compiler_params=params(),
        cost_estimate=cost(0.3),
        name="all_pieces",
    )(flags, own, *received)


def head_columns(flags, weight, turned):
    def kernel(flags_ref, weight_ref, turned_ref, *refs):
        out_refs, sems = refs[:4], refs[4]
        copies = []
        for k, out_ref in enumerate(out_refs):
            member = jnp.minimum((flags_ref[4] + k) % 4, 2)
            at = pl.ds(pl.multiple_of(member * 384, 128), 384)
            copies.append(pltpu.make_async_copy(weight_ref.at[:, at], out_ref.at[pl.ds(0, 48), :], sems.at[k]))
            copies.append(pltpu.make_async_copy(turned_ref, out_ref.at[pl.ds(48, 48), :], sems.at[4 + k]))
        for copy in copies:
            copy.start()
        for copy in copies:
            copy.wait()

    return pl.pallas_call(
        kernel,
        out_shape=(jax.ShapeDtypeStruct((96, 384), BF),) * 4,
        in_specs=[SMEM, HBM, ANY],
        out_specs=(FULL,) * 4,
        scratch_shapes=[pltpu.SemaphoreType.DMA((8,))],
        compiler_params=params(),
        cost_estimate=cost(0.3),
        name="head_columns",
    )(flags, weight, turned)


def by_z_hi(flags, blocks):
    def kernel(flags_ref, b0, b1, b3, b2, upper_ref, lower_ref):
        for k, block in enumerate((b0, b1, b2, b3)):
            at = pl.ds(pl.multiple_of((flags_ref[4] + 4 - k) % 4 * 48, 16), 48)
            upper_ref[at, :] = block[0:48, :]
            lower_ref[at, :] = block[48:96, :]

    return pl.pallas_call(
        kernel,
        out_shape=(jax.ShapeDtypeStruct((192, 384), BF),) * 2,
        in_specs=[SMEM] + [FULL] * 4,
        out_specs=(FULL,) * 2,
        compiler_params=params(),
        cost_estimate=cost(0.5),
        name="by_z_hi",
    )(flags, *blocks)


def lower(arrays):
    def kernel(*refs):
        for i, ref in enumerate(refs[:-1]):
            refs[-1][i * 192 : (i + 1) * 192, :] = ref[768:960, :]

    return pl.pallas_call(
        kernel,
        out_shape=jax.ShapeDtypeStruct((768, 384), BF),
        in_specs=[FULL] * 4,
        out_specs=FULL,
        compiler_params=params(),
        cost_estimate=cost(0.4),
        name="lower",
    )(*arrays)


def pieces(mine, other):
    def kernel(mine_ref, other_ref, *out_refs):
        for i, out_ref in enumerate(out_refs):
            out_ref[0:192, :] = mine_ref[i * 192 : (i + 1) * 192, :]
            out_ref[192:384, :] = other_ref[i * 192 : (i + 1) * 192, :]

    return pl.pallas_call(
        kernel,
        out_shape=(jax.ShapeDtypeStruct((384, 128), BF),) * 4,
        in_specs=[FULL] * 2,
        out_specs=(FULL,) * 4,
        compiler_params=params(),
        cost_estimate=cost(0.3),
        name="pieces",
    )(mine, other)


def rows_of(parts):
    arrays, counts = zip(*parts)

    def kernel(*refs):
        start = 0
        for count, ref in zip(counts, refs):
            refs[-1][start : start + count, :] = ref[0:count, :]
            start += count

    return pl.pallas_call(
        kernel,
        out_shape=jax.ShapeDtypeStruct((sum(counts), arrays[0].shape[1]), arrays[0].dtype),
        in_specs=[FULL] * len(arrays),
        out_specs=FULL,
        compiler_params=params(),
        cost_estimate=cost(0.4),
        name="rows_of",
    )(*arrays)


def over(arrays):
    return rows_of([(array, array.shape[0]) for array in arrays])


def after(value, *others):
    return lax.optimization_barrier((value, *others))[0]


def together(*values):
    return lax.optimization_barrier(values)


def body(tokens, prompt, prompt_mask, shift_vec, scale_vec, gate_vec, qkv_weight, query_gain, key_gain, out_weight):
    seq, head = lax.axis_index("seq"), lax.axis_index("head")
    y, x, z_hi, z_lo, core = seq // 16, (seq // 4) % 4, seq % 4, head // 2, head % 2
    flags = jnp.stack([z_lo, core, y, x, z_hi]).astype(jnp.int32)
    shift, gain = shift_vec[None], scale_vec[None]
    prompt_weight = lax.dynamic_slice(prompt_mask, (64 * y,), (64,)).astype(F32)
    prompt_weight = jnp.broadcast_to(prompt_weight[:, None], (64, 128))

    def along(k, core_x):
        return lambda y, x, z, c: (y, x + k, z, c) if c == core_x else (y + k, x, z, c)

    rows = head_columns(flags, qkv_weight, jnp.transpose(out_weight))
    rows = [rows[0]] + [send(rows[k], lambda y, x, z, c: (y, x, z + 2 * k, c)) for k in (1, 3, 2)]
    sibling, a1, *rows = together(to_sibling(tokens), round_z(tokens), *rows)

    column, out_column = by_z_hi(flags, rows)
    line = [send(column, along(k, 0)) for k in (1, 3, 2)]
    swap = [(d, device_at(d % 4, x, z // 2 * 2 + y // 2, y % 2)) for d in range(256) for y, x, z, c in [place(d)]]
    out_column = lax.ppermute(out_column, AX, swap)
    ring2, column, out_column, *line = together(round_z(over([a1, sibling])), column, out_column, *line)

    line = over([column] + line + [out_column])
    prompt_inputs = modulate_prompt(after(prompt, line), flags, shift, gain)
    weight1, weight3 = [send(line, along(k, 1)) for k in (1, 3)]
    ring3, line, weight1, weight3, prompt_inputs, prompt_weight = together(
        round_z(ring2), line, weight1, weight3, prompt_inputs, prompt_weight
    )

    rows1 = modulate_block((tokens, sibling, a1, ring2, ring3), first_blocks, flags, shift, gain, 3)
    ring4, weight2, rows1 = together(round_z(ring3), send(line, along(2, 1)), rows1)

    other = to_sibling(rows_of([(ring2, 192), (ring3, 384), (ring4, 384)]))
    sibling1 = to_sibling(rows1)
    weight_pieces = [line, weight1, weight3, weight2]
    out_line = lower(weight_pieces)
    out1, out3 = [send(out_line, along(k, 0)) for k in (1, 3)]
    rows3 = modulate_block((ring2, ring3, ring4, other), third_blocks, flags, shift, gain)
    rows4 = modulate_block((ring3, ring4, other), last_blocks, flags, shift, gain)
    inputs = [rows1, sibling1, rows3, rows4]
    q, kv, pk, pvt = project(flags, inputs, prompt_inputs, weight_pieces, query_gain[None], key_gain[None])

    q, kv, out1, out3, out_line = together(q, kv, out1, out3, out_line)
    kv1, kv3 = [send(kv, lambda y, x, z, c: (y, x + n, z, c)) for n in (1, 3)]
    q1, q3 = [send(q, lambda y, x, z, c: (y + n, x, z, c)) for n in (1, 3)]
    kv1, kv3, q1, q3 = together(kv1, kv3, q1, q3)
    kv2 = send(after(kv, kv1), lambda y, x, z, c: (y, x + 2, z, c))
    q2 = send(after(q, kv1), lambda y, x, z, c: (y + 2, x, z, c))
    prompt_parts = (pk, pvt, prompt_weight)
    sums = attend((q1, q3, q), ((kv,), (kv1,), (kv3,)), prompt_parts, (), False)
    q2, kv2, *sums = together(q2, kv2, *sums)
    (part2,) = attend((q2,), ((kv,), (kv1,), (kv3,), (kv2,)), prompt_parts, (), True)
    part1, part3, part0 = attend((q1, q3, q), ((kv2,),), (), sums, True)
    parts = [part0] + [send(p, lambda y, x, z, c: (y - n, x, z, c)) for n, p in ((2, part2), (1, part1), (3, part3))]
    attended = combine(parts)

    def turn(n):
        step = {0: lambda low: 0, 1: lambda low: -1 + 2 * low, 2: lambda low: 1 - 2 * low, 3: lambda low: 2}[n]
        ends = []
        for d in range(256):
            y, x, z, c = place(d)
            ends.append((d, device_at(y, x, (z // 2 + step(z % 2)) * 2 + c, z % 2)))
        return [(s, t) for s, t in ends if s != t]

    parts = pieces(attended, to_sibling(attended))
    near = [lax.ppermute(parts[n], AX, turn(n)) for n in (0, 1, 2, 3)]
    out2 = send(after(out_line, attended), along(2, 0))
    *near, out2 = together(*near, out2)
    near = all_pieces(flags, parts[0], near)
    return project_out(flags, near, to_sibling(near), [out_line, out1, out3, out2], gate_vec[None])


def solution(mesh):
    placed = (P("seq", "head"), P(), P(), P(), P(), P("head"), P("seq", "head"), P(), P(), P("head", "seq"))
    return jax.shard_map(body, mesh=mesh, in_specs=placed, out_specs=P("seq", "head"), check_vma=False)
```

```python
import math

import jax
import jax.numpy as jnp
from jax import lax
from jax.experimental import pallas as pl
from jax.experimental.pallas import tpu as pltpu
from jax.sharding import PartitionSpec as P

AX = ("seq", "head")
ORDER = (0, 1, 3, 2)
BF = jnp.bfloat16
F32 = jnp.float32
NT = (((1,), (1,)), ((), ()))
EXP2_SCALE = math.log2(math.e) / math.sqrt(128.0)
VMEM = 20 << 20
ANY = pl.BlockSpec(memory_space=pl.ANY)
SMEM = pl.BlockSpec(memory_space=pltpu.SMEM)
FULL = pl.BlockSpec(memory_space=pltpu.VMEM)
HBM = pl.BlockSpec(memory_space=pltpu.HBM)


def place(device):
    seq, head = divmod(device, 4)
    return seq // 16, (seq // 4) % 4, (seq % 4) * 2 + head // 2, head % 2


def device_at(y, x, z, core):
    y, x, z = y % 4, x % 4, z % 8
    return (y * 16 + x * 4 + z // 2) * 4 + (z % 2) * 2 + core


def send(value, target):
    pairs = [(d, device_at(*target(*place(d)))) for d in range(256)]
    return lax.ppermute(value, AX, pairs)


def to_sibling(value):
    return send(value, lambda y, x, z, c: (y, x, z, 1 - c))


def round_z(value):
    return send(value, lambda y, x, z, c: (y, x, z + 1 - 2 * c, c))


def cost(microseconds):
    return pl.CostEstimate(flops=0, bytes_accessed=int(microseconds * 3e6), transcendentals=0)


def params():
    return pltpu.CompilerParams(vmem_limit_bytes=VMEM)


def first_blocks(z_lo, core):
    near = z_lo != core
    chips = [[(0, 0), (1, 0)], [(2, 0), (3, 192)], [(3, 0), (4, 192)]]
    first, second = chips[0:2] if near else chips[1:3]
    if (z_lo == 1) == near:
        first, second = second, first
    return [chip[f ^ core] for chip in (first, second) for f in (0, 1)]


def third_blocks(z_lo, core):
    mine = [[(0, 0), (1, 192)], [(1, 0), (2, 192)]]
    other = [[(3, 0), (3, 384)], [(3, 192), (3, 768)]]
    near = z_lo != core
    first, second = [[chip[f ^ core if near else f ^ core ^ 1] for f in (0, 1)] for chip in (mine if near else other)]
    return first + second if z_lo == 0 else second + first


def last_blocks(z_lo, core):
    far = z_lo == core
    third = [[(0, 0), (1, 192)][f ^ core] if far else [(2, 192), (2, 768)][f ^ core ^ 1] for f in (0, 1)]
    fourth = [(1, 0) if f == core else (2, 576) for f in (0, 1)]
    return fourth + third if z_lo == 0 else third + fourth


def modulate_rows(rows, step, load, shift_ref, gain_ref, out_ref):
    @pl.loop(0, rows // step)
    def _(i):
        at = pl.ds(pl.multiple_of(i * step, step), step)
        total = jnp.zeros((step, 128), F32)
        for b in range(24):
            total = total + load(at, b)
        center = jnp.sum(total, axis=1, keepdims=True) * (1.0 / 3072)
        total = jnp.zeros((step, 128), F32)
        for b in range(24):
            value = load(at, b) - center
            total = total + value * value
        scale = lax.rsqrt(jnp.sum(total, axis=1, keepdims=True) * (1.0 / 3072) + 1e-06)
        for b in range(24):
            cols = slice(b * 128, (b + 1) * 128)
            out_ref[at, cols] = ((load(at, b) - center) * scale * (1.0 + gain_ref[:, cols]) + shift_ref[:, cols]).astype(BF)


def modulate_block(sources, choose, flags, shift, gain, far_sources=0):
    count = len(sources)

    def kernel(flags_ref, shift_ref, gain_ref, *refs):
        out_ref, buf, sems = refs[count:]
        for z_lo in (0, 1):
            for core in (0, 1):

                @pl.when((flags_ref[0] == z_lo) & (flags_ref[1] == core))
                def _():
                    copies = []
                    for b, source in enumerate(choose(z_lo, core)):
                        source, start = source
                        cols = slice(b * 768, (b + 1) * 768)
                        if source < far_sources:
                            copies.append(pltpu.make_async_copy(refs[source], buf.at[:, cols], sems.at[b]))
                            copies[-1].start()
                        else:
                            buf[:, cols] = refs[source][start : start + 192, :]
                    for copy in copies:
                        copy.wait()

        load = lambda at, b: buf[at, b * 128 : (b + 1) * 128].astype(F32)
        modulate_rows(192, 96, load, shift_ref, gain_ref, out_ref)

    return pl.pallas_call(
        kernel,
        out_shape=jax.ShapeDtypeStruct((192, 3072), BF),
        in_specs=[SMEM, FULL, FULL] + [HBM] * far_sources + [FULL] * (count - far_sources),
        out_specs=FULL,
        scratch_shapes=[pltpu.VMEM((192, 3072), BF), pltpu.SemaphoreType.DMA((4,))],
        compiler_params=params(),
        cost_estimate=cost(6),
        name="modulate",
    )(flags, shift, gain, *sources)


def modulate_prompt(prompt, flags, shift, gain):
    def kernel(flags_ref, shift_ref, gain_ref, prompt_ref, out_ref, buf, sem):
        at = pl.multiple_of(flags_ref[2] * 64, 64)
        copy = pltpu.make_async_copy(prompt_ref.at[pl.ds(at, 64), :], buf, sem)
        copy.start()
        copy.wait()
        load = lambda rows, b: buf[rows, b * 128 : (b + 1) * 128].astype(F32)
        modulate_rows(64, 64, load, shift_ref, gain_ref, out_ref)

    return pl.pallas_call(
        kernel,
        out_shape=jax.ShapeDtypeStruct((64, 3072), BF),
        in_specs=[SMEM, FULL, FULL, HBM],
        out_specs=FULL,
        scratch_shapes=[pltpu.VMEM((64, 3072), BF), pltpu.SemaphoreType.DMA],
        compiler_params=params(),
        cost_estimate=cost(6),
        name="modulate_prompt",
    )(flags, shift, gain, prompt)


def head_norm(values, gain):
    power = jnp.mean(values * values, axis=1, keepdims=True)
    return (values * lax.rsqrt(power + 1e-06) * gain).astype(BF)


def gathered_blocks(flags_ref, pieces, x_inside):
    core, y, x = flags_ref[1], flags_ref[2], flags_ref[3]
    for outer, piece in enumerate(pieces):
        for inner in range(4):
            dx = jnp.where(core == x_inside, ORDER[inner], ORDER[outer])
            dy = jnp.where(core == x_inside, ORDER[outer], ORDER[inner])
            block = ((y + 4 - dy) % 4) * 4 + (x + 4 - dx) % 4
            yield block, piece[inner * 192 : (inner + 1) * 192, :]


def project(flags, inputs, prompt_inputs, weight_pieces, query_gain, key_gain):
    def kernel(flags_ref, qg_ref, kg_ref, x0, x1, x2, x3, xp, w0, w1, w2, w3, q_ref, kv_ref, pk_ref, pvt_ref, w, part):
        for block, source in gathered_blocks(flags_ref, (w0, w1, w2, w3), 0):
            w[pl.ds(pl.multiple_of(block * 192, 192), 192), :] = source
        near = flags_ref[0] != flags_ref[1]
        for i, rows in enumerate((x0, x1)):
            at = pl.ds(pl.multiple_of(jnp.where(near, i, 1 - i) * 192, 192), 192)
            part[at, :] = jnp.dot(rows[...], w[...], preferred_element_type=F32)
        part[384:576, :] = jnp.dot(x2[...], w[...], preferred_element_type=F32)
        part[576:768, :] = jnp.dot(x3[...], w[...], preferred_element_type=F32)
        part[768:832, :] = jnp.dot(xp[...], w[...], preferred_element_type=F32)
        part[832:896, :] = jnp.zeros((64, 384), F32)
        for i in range(6):
            at = slice(i * 128, (i + 1) * 128)
            q_ref[at, :] = head_norm(part[at, :128], qg_ref[...])
            kv_ref[at, :] = head_norm(part[at, 128:256], kg_ref[...])
            kv_ref[768 + i * 128 : 896 + i * 128, :] = jnp.transpose(part[at, 256:]).astype(BF)
        pk_ref[...] = head_norm(part[768:832, 128:256], kg_ref[...])
        pvt_ref[...] = jnp.transpose(part[768:896, 256:])[:, :64].astype(BF)

    shape = jax.ShapeDtypeStruct
    return pl.pallas_call(
        kernel,
        out_shape=(shape((768, 128), BF), shape((1536, 128), BF), shape((64, 128), BF), shape((128, 64), BF)),
        in_specs=[SMEM] + [FULL] * 11,
        out_specs=(FULL,) * 4,
        scratch_shapes=[pltpu.VMEM((3072, 384), BF), pltpu.VMEM((896, 384), F32)],
        compiler_params=params(),
        cost_estimate=cost(6),
        name="project",
    )(flags, query_gain, key_gain, *inputs, prompt_inputs, *weight_pieces)


def attend(queries, pairs, prompt, sums, last):
    tile = 768
    n, m = len(queries), len(pairs)

    def kernel(*refs):
        refs = list(refs)
        q_refs, rest = refs[:n], refs[n:]
        kv_refs = []
        for pair in pairs:
            kv_refs.append((rest[0], rest[len(pair) - 1], 768 * (len(pair) == 1)))
            rest = rest[len(pair) :]
        if prompt:
            pk, pv, pw = rest[:3]
            rest = rest[3:]
        sum_refs = rest[: len(sums)]
        out_refs = rest[len(sums) :]
        for i in range(n):
            for t in range(768 // tile):
                at = slice(t * tile, (t + 1) * tile)
                query = q_refs[i][at, :]
                if sums:
                    numer, denom = sum_refs[i][0:128, at], sum_refs[i][128:136, at]
                else:
                    numer, denom = jnp.zeros((128, tile), F32), jnp.zeros((8, tile), F32)
                for keys, values, start in kv_refs:
                    scores = lax.dot_general(keys[0:768, :], query, NT, preferred_element_type=F32)
                    expon = jnp.exp2(scores * EXP2_SCALE)
                    denom = denom + jnp.sum(expon.reshape(96, 8, tile), axis=0)
                    value = jnp.concatenate([values[start + 128 * j : start + 128 * (j + 1), :] for j in range(6)], axis=1)
                    numer = numer + jnp.dot(value, expon.astype(BF), preferred_element_type=F32)
                if prompt:
                    scores = lax.dot_general(pk[...], query, NT, preferred_element_type=F32)
                    expon = jnp.exp2(scores * EXP2_SCALE) * pw[:, :1]
                    denom = denom + jnp.sum(expon.reshape(8, 8, tile), axis=0)
                    numer = numer + jnp.dot(pv[...], expon.astype(BF), preferred_element_type=F32)
                if last:
                    total = jnp.sum(denom, axis=0, keepdims=True)
                    high = total.astype(BF).astype(F32)
                    out_refs[i][0:128, at] = numer.astype(BF)
                    low = jnp.concatenate([high, total - high, jnp.zeros((14, tile), F32)], axis=0)
                    out_refs[i][128:144, at] = low.astype(BF)
                else:
                    out_refs[i][0:128, at] = numer
                    out_refs[i][128:136, at] = denom

    out = jax.ShapeDtypeStruct((144, 768), BF) if last else jax.ShapeDtypeStruct((136, 768), F32)
    args = [*queries, *[part for pair in pairs for part in pair], *prompt, *sums]
    return pl.pallas_call(
        kernel,
        out_shape=(out,) * n,
        in_specs=[FULL] * len(args),
        out_specs=(FULL,) * n,
        compiler_params=params(),
        cost_estimate=cost(0.7 * n * m),
        name="attend",
    )(*args)


def combine(parts):
    def kernel(a, b, c, d, out_ref):
        parts = [r[...].astype(F32) for r in (a, b, c, d)]
        total = parts[0] + parts[1] + parts[2] + parts[3]
        denom = total[128:129, :] + total[129:130, :]
        out_ref[...] = jnp.transpose(total[:128, :] / denom).astype(BF)

    return pl.pallas_call(
        kernel,
        out_shape=jax.ShapeDtypeStruct((768, 128), BF),
        in_specs=[FULL] * 4,
        out_specs=FULL,
        compiler_params=params(),
        cost_estimate=cost(0.5),
        name="combine",
    )(*parts)


def project_out(flags, near, far, weight_pieces, gate):
    def kernel(flags_ref, near_ref, far_ref, w0, w1, w2, w3, gate_ref, out_ref, rows, weight):
        z_lo, core, z_hi = flags_ref[0], flags_ref[1], flags_ref[4]
        for block, source in gathered_blocks(flags_ref, (w0, w1, w2, w3), 1):
            weight[block // 4, pl.ds(pl.multiple_of(block % 4 * 192, 192), 192), :] = source

        def put(low, r, ref, start):
            member = (z_hi + 4 + {0: 0, 1: 1 - 2 * low, 2: 2 * low - 1, 3: 2}[r]) % 4

            @pl.when(member < 3)
            def _():
                for half in (0, 1):
                    head_group = low * 2 + (z_lo + half) % 2
                    at = pl.multiple_of(head_group * 384 + member * 128, 128)
                    rows[:, pl.ds(at, 128)] = ref[start + half * 192 : start + half * 192 + 192, :]

        for r in (0, 1, 2, 3):
            put(core, r, near_ref, r * 384)
            put(1 - core, r, far_ref, r * 384)
        total = jnp.zeros((192, 768), F32)
        for h in range(4):
            total = total + lax.dot_general(rows[:, h * 384 : (h + 1) * 384], weight[h], NT, preferred_element_type=F32)
        out_ref[...] = (total * gate_ref[...]).astype(BF)

    return pl.pallas_call(
        kernel,
        out_shape=jax.ShapeDtypeStruct((192, 768), BF),
        in_specs=[SMEM] + [FULL] * 7,
        out_specs=FULL,
        scratch_shapes=[pltpu.VMEM((192, 1536), BF), pltpu.VMEM((4, 768, 384), BF)],
        compiler_params=params(),
        cost_estimate=cost(3),
        name="project_out",
    )(flags, near, far, *weight_pieces, gate)


def all_pieces(flags, own, received):
    def kernel(flags_ref, own_ref, *refs):
        out_ref = refs[4]

        @pl.when(flags_ref[0] == flags_ref[1])
        def _():
            out_ref[0:384, :] = own_ref[...]

        @pl.when(flags_ref[0] != flags_ref[1])
        def _():
            out_ref[0:384, :] = refs[0][...]

        for r in (1, 2, 3):
            out_ref[r * 384 : (r + 1) * 384, :] = refs[r][...]

    return pl.pallas_call(
        kernel,
        out_shape=jax.ShapeDtypeStruct((1536, 128), BF),
        in_specs=[SMEM] + [FULL] * 5,
        out_specs=FULL,
        compiler_params=params(),
        cost_estimate=cost(0.3),
        name="all_pieces",
    )(flags, own, *received)


def head_columns(flags, weight, turned):
    def kernel(flags_ref, weight_ref, turned_ref, *refs):
        out_refs, sems = refs[:4], refs[4]
        copies = []
        for k, out_ref in enumerate(out_refs):
            member = jnp.minimum((flags_ref[4] + k) % 4, 2)
            at = pl.ds(pl.multiple_of(member * 384, 128), 384)
            copies.append(pltpu.make_async_copy(weight_ref.at[:, at], out_ref.at[pl.ds(0, 48), :], sems.at[k]))
            copies.append(pltpu.make_async_copy(turned_ref, out_ref.at[pl.ds(48, 48), :], sems.at[4 + k]))
        for copy in copies:
            copy.start()
        for copy in copies:
            copy.wait()

    return pl.pallas_call(
        kernel,
        out_shape=(jax.ShapeDtypeStruct((96, 384), BF),) * 4,
        in_specs=[SMEM, HBM, ANY],
        out_specs=(FULL,) * 4,
        scratch_shapes=[pltpu.SemaphoreType.DMA((8,))],
        compiler_params=params(),
        cost_estimate=cost(0.3),
        name="head_columns",
    )(flags, weight, turned)


def by_z_hi(flags, blocks):
    def kernel(flags_ref, b0, b1, b3, b2, upper_ref, lower_ref):
        for k, block in enumerate((b0, b1, b2, b3)):
            at = pl.ds(pl.multiple_of((flags_ref[4] + 4 - k) % 4 * 48, 16), 48)
            upper_ref[at, :] = block[0:48, :]
            lower_ref[at, :] = block[48:96, :]

    return pl.pallas_call(
        kernel,
        out_shape=(jax.ShapeDtypeStruct((192, 384), BF),) * 2,
        in_specs=[SMEM] + [FULL] * 4,
        out_specs=(FULL,) * 2,
        compiler_params=params(),
        cost_estimate=cost(0.5),
        name="by_z_hi",
    )(flags, *blocks)


def lower(arrays):
    def kernel(*refs):
        for i, ref in enumerate(refs[:-1]):
            refs[-1][i * 192 : (i + 1) * 192, :] = ref[768:960, :]

    return pl.pallas_call(
        kernel,
        out_shape=jax.ShapeDtypeStruct((768, 384), BF),
        in_specs=[FULL] * 4,
        out_specs=FULL,
        compiler_params=params(),
        cost_estimate=cost(0.4),
        name="lower",
    )(*arrays)


def pieces(mine, other):
    def kernel(mine_ref, other_ref, *out_refs):
        for i, out_ref in enumerate(out_refs):
            out_ref[0:192, :] = mine_ref[i * 192 : (i + 1) * 192, :]
            out_ref[192:384, :] = other_ref[i * 192 : (i + 1) * 192, :]

    return pl.pallas_call(
        kernel,
        out_shape=(jax.ShapeDtypeStruct((384, 128), BF),) * 4,
        in_specs=[FULL] * 2,
        out_specs=(FULL,) * 4,
        compiler_params=params(),
        cost_estimate=cost(0.3),
        name="pieces",
    )(mine, other)


def rows_of(parts):
    arrays, counts = zip(*parts)

    def kernel(*refs):
        start = 0
        for count, ref in zip(counts, refs):
            refs[-1][start : start + count, :] = ref[0:count, :]
            start += count

    return pl.pallas_call(
        kernel,
        out_shape=jax.ShapeDtypeStruct((sum(counts), arrays[0].shape[1]), arrays[0].dtype),
        in_specs=[FULL] * len(arrays),
        out_specs=FULL,
        compiler_params=params(),
        cost_estimate=cost(0.4),
        name="rows_of",
    )(*arrays)


def over(arrays):
    return rows_of([(array, array.shape[0]) for array in arrays])


def after(value, *others):
    return lax.optimization_barrier((value, *others))[0]


def together(*values):
    return lax.optimization_barrier(values)


def body(tokens, prompt, prompt_mask, shift_vec, scale_vec, gate_vec, qkv_weight, query_gain, key_gain, out_weight):
    seq, head = lax.axis_index("seq"), lax.axis_index("head")
    y, x, z_hi, z_lo, core = seq // 16, (seq // 4) % 4, seq % 4, head // 2, head % 2
    flags = jnp.stack([z_lo, core, y, x, z_hi]).astype(jnp.int32)
    shift, gain = shift_vec[None], scale_vec[None]
    prompt_weight = lax.dynamic_slice(prompt_mask, (64 * y,), (64,)).astype(F32)
    prompt_weight = jnp.broadcast_to(prompt_weight[:, None], (64, 128))

    def along(k, core_x):
        return lambda y, x, z, c: (y, x + k, z, c) if c == core_x else (y + k, x, z, c)

    rows = head_columns(flags, qkv_weight, jnp.transpose(out_weight))
    rows = [rows[0]] + [send(rows[k], lambda y, x, z, c: (y, x, z + 2 * k, c)) for k in (1, 3, 2)]
    sibling, a1, *rows = together(to_sibling(tokens), round_z(tokens), *rows)

    column, out_column = by_z_hi(flags, rows)
    line = [send(column, along(k, 0)) for k in (1, 3, 2)]
    swap = [(d, device_at(d % 4, x, z // 2 * 2 + y // 2, y % 2)) for d in range(256) for y, x, z, c in [place(d)]]
    out_column = lax.ppermute(out_column, AX, swap)
    ring2, column, out_column, *line = together(round_z(over([a1, sibling])), column, out_column, *line)

    line = over([column] + line + [out_column])
    prompt_inputs = modulate_prompt(after(prompt, line), flags, shift, gain)
    weight1, weight3 = [send(line, along(k, 1)) for k in (1, 3)]
    ring3, line, weight1, weight3, prompt_inputs, prompt_weight = together(
        round_z(ring2), line, weight1, weight3, prompt_inputs, prompt_weight
    )

    rows1 = modulate_block((tokens, sibling, a1, ring2, ring3), first_blocks, flags, shift, gain, 3)
    ring4, weight2, rows1 = together(round_z(ring3), send(line, along(2, 1)), rows1)

    other = to_sibling(rows_of([(ring2, 192), (ring3, 384), (ring4, 384)]))
    sibling1 = to_sibling(rows1)
    weight_pieces = [line, weight1, weight3, weight2]
    out_line = lower(weight_pieces)
    out1, out3 = [send(out_line, along(k, 0)) for k in (1, 3)]
    rows3 = modulate_block((ring2, ring3, ring4, other), third_blocks, flags, shift, gain)
    rows4 = modulate_block((ring3, ring4, other), last_blocks, flags, shift, gain)
    inputs = [rows1, sibling1, rows3, rows4]
    q, kv, pk, pvt = project(flags, inputs, prompt_inputs, weight_pieces, query_gain[None], key_gain[None])

    q, kv, out1, out3, out_line = together(q, kv, out1, out3, out_line)
    kv1, kv3 = [send(kv, lambda y, x, z, c: (y, x + n, z, c)) for n in (1, 3)]
    q1, q3 = [send(q, lambda y, x, z, c: (y + n, x, z, c)) for n in (1, 3)]
    kv1, kv3, q1, q3 = together(kv1, kv3, q1, q3)
    kv2 = send(after(kv, kv1), lambda y, x, z, c: (y, x + 2, z, c))
    q2 = send(after(q, kv1), lambda y, x, z, c: (y + 2, x, z, c))
    prompt_parts = (pk, pvt, prompt_weight)
    sums = attend((q1, q3, q), ((kv,), (kv1,), (kv3,)), prompt_parts, (), False)
    q2, kv2, *sums = together(q2, kv2, *sums)
    (part2,) = attend((q2,), ((kv,), (kv1,), (kv3,), (kv2,)), prompt_parts, (), True)
    part1, part3, part0 = attend((q1, q3, q), ((kv2,),), (), sums, True)
    parts = [part0] + [send(p, lambda y, x, z, c: (y - n, x, z, c)) for n, p in ((2, part2), (1, part1), (3, part3))]
    attended = combine(parts)

    def turn(n):
        step = {0: lambda low: 0, 1: lambda low: -1 + 2 * low, 2: lambda low: 1 - 2 * low, 3: lambda low: 2}[n]
        ends = []
        for d in range(256):
            y, x, z, c = place(d)
            ends.append((d, device_at(y, x, (z // 2 + step(z % 2)) * 2 + c, z % 2)))
        return [(s, t) for s, t in ends if s != t]

    parts = pieces(attended, to_sibling(attended))
    near = [lax.ppermute(parts[n], AX, turn(n)) for n in (0, 1, 2, 3)]
    out2 = send(after(out_line, attended), along(2, 0))
    near = together(*near)
    near = all_pieces(flags, parts[0], near)
    return project_out(flags, near, to_sibling(near), [out_line, out1, out3, out2], gate_vec[None])


def solution(mesh):
    placed = (P("seq", "head"), P(), P(), P(), P(), P("head"), P("seq", "head"), P(), P(), P("head", "seq"))
    return jax.shard_map(body, mesh=mesh, in_specs=placed, out_specs=P("seq", "head"), check_vma=False)
```
